512 devices in a mesh: dp: 64 (over z, x, y_hi), feat: 8 (over y_lo, core).
Axes of the slice: x: 4, y: 8 (y_hi: 2, y_lo: 4; y = y_hi * 4 + y_lo), z: 8, core: 2. Of those that a mesh axis runs over, the one named last changes fastest.
Arguments:
- student: bfloat16 [8192, 768], P('dp'), may hold values from -40 to 40
- proj_weight: bfloat16 [768, 8192], P(None, 'feat'), may hold values from -6 to 6
- teacher: bfloat16 [8192, 8192], P('dp', 'feat'), may hold values from -480 to 480
- anchors: int32 [24576], P('dp'), may hold values from 0 to 127
- pairs: int32 [2, 24576], P(None, 'dp'), may hold values from 0 to 383
Outputs:
- grad_w: float32 [768, 8192], P('dp', 'feat')
- grad_student: float32 [8192, 768], P('dp', 'feat')
The draws below stay inside these ranges and needn't reach their ends.
All inputs are finite; a program needn't handle non-finite values.
Results may differ from the reference program's by a relative error of at most 0.015.
Values may be sent and summed in bfloat16 or wider, within the bound.
No kernel may reach another device: no remote copies, remote signals or barrier semaphores. Data moves between devices by JAX's collectives and lax.ppermute only.
A program may use at most 64 MiB of HBM per device.

```python
import math
import jax
import jax.numpy as jnp
from jax import lax

DS = 768
F = 8192
ROWS = 128
STEPS = 3
TRIP = 384
TEXTS = 8192
TRIPLETS = 24576
N_DP = 64


def spread_columns(column_key, extent):
    rising = 3.0 ** (jnp.arange(extent, dtype=jnp.float32) / extent)
    return rising * jnp.exp(jax.random.uniform(column_key, (extent,), jnp.float32, 0.0, math.log(4.0)))


def draw_student(key, part):
    key = jax.random.fold_in(key, 11)
    base_key, rows_key, perm_key = jax.random.split(key, 3)
    block_total = TEXTS // ROWS
    width_block = DS // block_total
    values = jnp.clip(jax.random.normal(base_key, (TEXTS, DS), jnp.float32), -4.0, 4.0)
    scales = jnp.exp(jax.random.uniform(rows_key, (TEXTS, 1), jnp.float32, math.log(0.25), math.log(2.5)))
    owner_block = jax.random.permutation(perm_key, block_total)
    row_block = jnp.arange(TEXTS, dtype=jnp.int32) // ROWS
    col_block = jnp.arange(DS, dtype=jnp.int32) // width_block
    boosted = owner_block[row_block][:, None] == col_block[None, :]
    boost_factor = jnp.where(boosted, 4.0, 1.0)
    return (values * scales * boost_factor).astype(jnp.bfloat16)


def draw_proj_weight(key, part):
    key = jax.random.fold_in(key, 12)
    base_key, column_key = jax.random.split(key, 2)
    values = jnp.clip(jax.random.normal(base_key, (DS, F), jnp.float32), -4.0, 4.0)
    return (values * spread_columns(column_key, F)[None, :] / math.sqrt(DS)).astype(jnp.bfloat16)


def draw_teacher(key, part):
    key = jax.random.fold_in(key, 13)
    base_key, column_key, rows_key = jax.random.split(key, 3)
    values = jnp.clip(jax.random.normal(base_key, (TEXTS, F), jnp.float32), -4.0, 4.0)
    scales = jnp.exp(jax.random.uniform(rows_key, (TEXTS, 1), jnp.float32, 0.0, math.log(10.0)))
    return (values * scales * spread_columns(column_key, F)[None, :]).astype(jnp.bfloat16)


def set_ends(array, rng, low, high):
    dims = array.shape
    spot = [jax.random.randint(jax.random.fold_in(rng, axis), (), 0, dims[axis]) for axis in range(len(dims))]
    array = array.at[tuple(spot)].set(low)
    longest = dims.index(max(dims))
    spot[longest] = (spot[longest] + 1) % dims[longest]
    return array.at[tuple(spot)].set(high)


def setup_inputs(seed: int = 0) -> dict:
    key_list = jax.random.split(jax.random.key(seed), 6)
    return {
        "student": draw_student(jax.random.fold_in(key_list[5], 71), 0),
        "proj_weight": draw_proj_weight(jax.random.fold_in(key_list[5], 71), 0),
        "teacher": draw_teacher(jax.random.fold_in(key_list[5], 71), 0),
        "anchors": set_ends(jax.random.randint(key_list[3], (TRIPLETS,), 0, ROWS), jax.random.fold_in(key_list[3], 1), 0, ROWS - 1).astype(jnp.int32),
        "pairs": set_ends(jax.random.randint(key_list[4], (2, TRIPLETS), 0, STEPS * ROWS), jax.random.fold_in(key_list[4], 1), 0, (STEPS * ROWS) - 1).astype(jnp.int32),
    }


EPSILON = 1e-06
TEMPER = 50.0
MARGIN = 0.01
LOSS_SCALE = 1024.0

def row_products(left_mat, right_mat):
    return lax.dot_general(left_mat, right_mat, (((1,), (1,)), ((), ())), preferred_element_type=jnp.float32)

def column_products(left_mat, right_mat):
    return lax.dot_general(left_mat, right_mat, (((0,), (0,)), ((), ())), preferred_element_type=jnp.float32)

def relative_grad(sim_band, teach_band, anchor_rows, pair_cols):
    first_col = pair_cols[0]
    second_col = pair_cols[1]
    gap_student = sim_band[anchor_rows, first_col] - sim_band[anchor_rows, second_col]
    gap_teacher = teach_band[anchor_rows, first_col] - teach_band[anchor_rows, second_col]
    weight = jnp.tanh(TEMPER * gap_teacher)
    slopes = -weight * jax.nn.sigmoid(TEMPER * (MARGIN - weight * gap_student))
    gradient = 2.0 * (sim_band - teach_band)
    gradient = gradient.at[anchor_rows, first_col].add(slopes)
    gradient = gradient.at[anchor_rows, second_col].add(-slopes)
    return gradient

def reference(student, proj_weight, teacher, anchors, pairs):
    projected = jnp.dot(student, proj_weight, preferred_element_type=jnp.float32)
    teacher_wide = teacher.astype(jnp.float32)
    inv_proj = lax.rsqrt(lax.optimization_barrier(jnp.sum(projected * projected, 1)) + EPSILON)
    inv_teach = lax.rsqrt(lax.optimization_barrier(jnp.sum(teacher_wide * teacher_wide, 1)) + EPSILON)
    cosine = lax.optimization_barrier(jnp.sum(projected * teacher_wide, 1)) * inv_proj * inv_teach
    unit_rows = projected * inv_proj[:, None]
    student_unit = unit_rows.astype(jnp.bfloat16)
    teacher_unit = (teacher_wide * inv_teach[:, None]).astype(jnp.bfloat16)
    block_ids = jnp.arange(N_DP, dtype=jnp.int32)

    def forward_block(block_id):
        first_row = (block_id * ROWS).astype(jnp.int32)
        own_student = lax.dynamic_slice_in_dim(student_unit, first_row, ROWS, 0)
        own_teacher = lax.dynamic_slice_in_dim(teacher_unit, first_row, ROWS, 0)
        sim_tiles = []
        teach_tiles = []
        partners = []
        for cycle_step in range(STEPS):
            partner_row = ((block_id + cycle_step) % N_DP * ROWS).astype(jnp.int32)
            partner_student = lax.dynamic_slice_in_dim(student_unit, partner_row, ROWS, 0)
            partner_teacher = lax.dynamic_slice_in_dim(teacher_unit, partner_row, ROWS, 0)
            partners.append(partner_student)
            sim_tiles.append(row_products(own_student, partner_student))
            teach_tiles.append(row_products(own_teacher, partner_teacher))
        sim_band = jnp.concatenate(sim_tiles, 1)
        teach_band = jnp.concatenate(teach_tiles, 1)
        block_anchors = lax.dynamic_slice_in_dim(anchors, (block_id * TRIP).astype(jnp.int32), TRIP, 0)
        block_pairs = lax.dynamic_slice_in_dim(pairs, (block_id * TRIP).astype(jnp.int32), TRIP, 1)
        gradient = relative_grad(sim_band, teach_band, block_anchors, block_pairs).astype(jnp.bfloat16)
        collected = jnp.zeros((ROWS, F), jnp.float32)
        for cycle_step in range(STEPS):
            band_tile = gradient[:, cycle_step * ROWS:(cycle_step + 1) * ROWS]
            collected = collected + jnp.dot(band_tile, partners[cycle_step], preferred_element_type=jnp.float32)
        return (gradient, collected)
    gradients, row_parts = lax.map(forward_block, block_ids)

    def return_block(block_id):
        collected = jnp.zeros((ROWS, F), jnp.float32)
        for cycle_step in range(STEPS):
            source = ((block_id - cycle_step) % N_DP).astype(jnp.int32)
            source_grad = lax.dynamic_index_in_dim(gradients, source, 0, keepdims=False)
            band_tile = source_grad[:, cycle_step * ROWS:(cycle_step + 1) * ROWS]
            source_rows = lax.dynamic_slice_in_dim(student_unit, (source * ROWS).astype(jnp.int32), ROWS, 0)
            collected = collected + column_products(band_tile, source_rows)
        return collected
    returned = lax.map(return_block, block_ids)
    unit_grad = (row_parts + returned).reshape(TEXTS, F)
    inner_part = lax.optimization_barrier(jnp.sum(unit_rows * unit_grad, 1))
    target = teacher_wide * inv_teach[:, None]
    proj_grad = (LOSS_SCALE * inv_proj[:, None] * (unit_grad - target + (cosine - inner_part)[:, None] * unit_rows)).astype(jnp.bfloat16)
    grad_w = column_products(student, proj_grad)
    grad_student = row_products(proj_grad, proj_weight)
    return (grad_w, grad_student)
```

```python
import functools

import jax
import jax.numpy as jnp
from jax import lax
from jax.experimental import pallas as pl
from jax.experimental.pallas import tpu as pltpu
from jax.sharding import Mesh, PartitionSpec as P

STEPS = 3
EPSILON = 1e-06
TEMPER = 50.0
MARGIN = 0.01
LOSS_SCALE = 1024.0

DP_SIZES = {64: (4, 8, 2), 8: (2, 2, 2)}
DP = ("z", "x", "yh")
LANES = 128
f32 = jnp.float32
bf16 = jnp.bfloat16
HIGHEST = lax.Precision.HIGHEST


def dot(left, right, contract, precision=None):
    return lax.dot_general(
        left, right, ((contract[:1], contract[1:]), ((), ())),
        preferred_element_type=f32, precision=precision,
    )


def passed_along(array, by):
    peers = lax.axis_size(DP)
    return lax.ppermute(array, DP, [(i, (i + by) % peers) for i in range(peers)])


def band_kernel(parts, norms, ids, out):
    rows = parts.shape[1]
    band = norms.shape[1]
    sums = jnp.sum(parts[...], 0)
    inv_proj = norms[0:1, :]
    inv_teach = norms[1:2, :]
    row_id = lax.broadcasted_iota(jnp.int32, (rows, band), 0)
    anchor = (ids[0:1, :] == row_id).astype(f32)
    own = (ids[3:4, :] == row_id).astype(f32)
    row_proj = jnp.sum(own * inv_proj, 1, keepdims=True)
    row_teach = jnp.sum(own * inv_teach, 1, keepdims=True)
    sim = sums[:, :band] * (row_proj * inv_proj)
    teach = sums[:, band:] * (row_teach * inv_teach)
    col_id = lax.broadcasted_iota(jnp.int32, (band, band), 0)
    pick = (col_id == ids[1:2, :]).astype(f32) - (col_id == ids[2:3, :]).astype(f32)
    gap_s = jnp.sum(dot(sim, anchor, (0, 0), HIGHEST) * pick, 0, keepdims=True)
    gap_t = jnp.sum(dot(teach, anchor, (0, 0), HIGHEST) * pick, 0, keepdims=True)
    weight = jnp.tanh(TEMPER * gap_t)
    slope = -weight * jax.nn.sigmoid(TEMPER * (MARGIN - weight * gap_s))
    grad = 2.0 * (sim - teach) + dot(anchor * slope, pick, (1, 1), HIGHEST)
    product = grad * sim
    along = jnp.sum(product, 1, keepdims=True)
    inner = jnp.sum(product + along * own, 0, keepdims=True) * (inv_proj * inv_proj)
    inner_high = inner.astype(bf16)
    inner_low = (inner - inner_high.astype(f32)).astype(bf16)
    tail_id = lax.broadcasted_iota(jnp.int32, (16, band), 0)
    tail = jnp.where(
        tail_id == 0, inner_high.astype(f32), jnp.where(tail_id == 1, inner_low.astype(f32), 0.0)
    )
    out[0:rows, :] = (grad * (row_proj * inv_proj)).astype(bf16)
    out[rows : rows + 16, :] = tail.astype(bf16)


def spread_kernel(gathered, student_band, student_cols, student_pad, own, first, second, mixed):
    peers, height, band = gathered.shape
    rows = height - 16
    texts = peers * rows
    tile = gathered[:, 0:rows, :].reshape(texts, band)
    inner = jnp.sum(gathered[:, rows : rows + 16, :].astype(f32), (0, 1)).reshape(1, band)
    diagonal = lax.broadcasted_iota(jnp.int32, (band, band), 0) == lax.broadcasted_iota(
        jnp.int32, (band, band), 1
    )
    inner_col = jnp.sum(jnp.where(diagonal, inner, 0.0), 1, keepdims=True)

    def spread(values):
        direct = dot(tile, values, (1, 0))
        back = dot(tile, values[:texts], (0, 0)) - inner_col * values.astype(f32)
        return direct + back[:texts], back[texts:]

    head, rest = spread(student_cols[...])
    slab = jnp.concatenate([head, rest], 0).astype(bf16)
    mixed[...] = dot(student_pad[...], slab, (1, 0)).astype(bf16)
    head, rest = spread(student_band[...])
    own[...] = head
    first[...] = rest[:texts].astype(bf16)
    second[...] = rest[texts:].astype(bf16)


def one_hot_pad(features, sizes, padded, by_x):
    z_size, x_size, yh_size = sizes
    share = features // (z_size * x_size * yh_size)
    wide = padded if padded else share
    out = lax.broadcasted_iota(jnp.int32, (z_size * x_size * yh_size * wide, features), 0)
    feature = lax.broadcasted_iota(jnp.int32, out.shape, 1)
    place, offset = out // wide, out % wide
    if by_x:
        yh = place % yh_size
        z = (place // yh_size) % z_size
        x = place // (yh_size * z_size)
        place = (z * x_size + x) * yh_size + yh
    return ((feature == place * share + offset) & (offset < share)).astype(bf16)


def shards(student, proj_weight, teacher, anchors, pairs, *, sizes):
    z_size, x_size, yh_size = sizes
    n_dp = z_size * x_size * yh_size
    n_feat = lax.axis_size("feat")
    texts, features = student.shape
    width = teacher.shape[1]
    band = STEPS * texts
    rows = texts // n_feat
    share = features // n_dp
    padded = -(-share // 16) * 16
    groups = features // LANES
    feat = lax.axis_index("feat")

    packed = jnp.concatenate([teacher, student], 1)
    near = passed_along(packed, -1)
    far = passed_along(packed, -2)

    projected = dot(student, proj_weight, (1, 0))
    teacher_wide = teacher.astype(f32)
    proj_sq, teach_sq, cross = lax.psum(
        (
            jnp.sum(projected * projected, 1),
            jnp.sum(teacher_wide * teacher_wide, 1),
            jnp.sum(projected * teacher_wide, 1),
        ),
        "feat",
    )
    inv_proj = lax.rsqrt(proj_sq + EPSILON)
    inv_teach = lax.rsqrt(teach_sq + EPSILON)
    cosine = cross * inv_proj * inv_teach
    own_norms = jnp.stack([inv_proj, inv_teach])
    norms = jnp.concatenate(
        [own_norms, passed_along(own_norms, -1), passed_along(own_norms, -2)], 1
    )

    direct = (LOSS_SCALE * inv_proj)[:, None] * (
        (cosine * inv_proj)[:, None] * projected - inv_teach[:, None] * teacher_wide
    )
    regroup = dot(one_hot_pad(features, sizes, 0, True), student, (1, 1)).astype(bf16)
    direct_part = dot(regroup, direct.astype(bf16), (1, 0)).astype(bf16)
    direct_part = lax.all_to_all(
        direct_part.reshape(x_size, features // x_size, width), "x", 0, 0
    ).reshape(features, width)
    zy = z_size * yh_size
    row_out = lax.broadcasted_iota(jnp.int32, (zy * padded, features), 0)
    row_in = lax.broadcasted_iota(jnp.int32, (zy * padded, features), 1) % (zy * share)
    gather_rows = (
        (row_out // padded == row_in // share) & (row_out % padded == row_in % share)
    ).astype(bf16)
    direct_part = dot(gather_rows, direct_part, (1, 0)).astype(bf16)
    direct_part = lax.all_to_all(direct_part.reshape(zy, padded, width), ("z", "yh"), 0, 0)
    grad_w_direct = jnp.sum(direct_part.astype(f32), 0)

    student_band = jnp.concatenate([student, near[:, width:], far[:, width:]], 0)
    proj_own = projected.astype(bf16)
    proj_rest = dot(student_band[texts:], proj_weight, (1, 0)).astype(bf16)
    proj_band = jnp.concatenate([proj_own, proj_rest], 0)
    teach_band = jnp.concatenate([teacher, near[:, :width], far[:, :width]], 0)
    parts = jnp.concatenate(
        [dot(proj_own, proj_band, (1, 1)), dot(teacher, teach_band, (1, 1))], 1
    )
    parts = lax.all_to_all(parts.reshape(n_feat, rows, 2 * band), "feat", 0, 0)
    ids = jnp.concatenate(
        [
            anchors[None] - feat * rows,
            pairs,
            lax.broadcasted_iota(jnp.int32, (1, band), 1) - feat * rows,
            jnp.zeros((4, band), jnp.int32),
        ],
        0,
    )
    tile = pl.pallas_call(
        band_kernel,
        out_shape=jax.ShapeDtypeStruct((rows + 16, band), bf16),
        cost_estimate=pl.CostEstimate(flops=10**8, bytes_accessed=10**6, transcendentals=1000),
        name="band",
    )(parts, norms, ids)
    gathered = lax.all_gather(tile, "feat")

    student_pad = dot(one_hot_pad(features, sizes, padded, False), student_band, (1, 1)).astype(bf16)
    col_start = jnp.minimum(feat, groups - 1) * LANES
    student_cols = lax.dynamic_slice(student_band, (0, col_start), (band, LANES))
    student_cols = jnp.where(feat < groups, student_cols, jnp.zeros_like(student_cols))
    own, first, second, mixed = pl.pallas_call(
        spread_kernel,
        out_shape=(
            jax.ShapeDtypeStruct((texts, features), f32),
            jax.ShapeDtypeStruct((texts, features), bf16),
            jax.ShapeDtypeStruct((texts, features), bf16),
            jax.ShapeDtypeStruct((n_dp * padded, LANES), bf16),
        ),
        cost_estimate=pl.CostEstimate(flops=10**9, bytes_accessed=4 * 10**6, transcendentals=0),
        name="spread",
    )(gathered, student_band, student_cols, student_pad)

    mixed = lax.all_to_all(mixed.reshape(n_dp, padded, LANES), DP, 0, 0)
    mixed = jnp.sum(mixed.astype(f32), 0).astype(bf16)
    mixed = lax.all_gather(mixed, "feat")
    mixed = jnp.concatenate([mixed[g] for g in range(groups)], 1)
    grad_w = (grad_w_direct + LOSS_SCALE * dot(mixed, proj_weight, (1, 0)))[:share]

    spread = own + passed_along(first, 1).astype(f32) + passed_along(second, 2).astype(f32)
    proj_grad = (direct + LOSS_SCALE * dot(spread.astype(bf16), proj_weight, (1, 0))).astype(bf16)
    back = dot(proj_weight, proj_grad, (1, 1)).astype(bf16)
    back = lax.all_to_all(back.reshape(n_feat, features // n_feat, texts), "feat", 0, 0)
    grad_student = jnp.sum(back.astype(f32), 0).T
    return (grad_w, grad_student)


def solution(mesh):
    n_dp, n_feat = mesh.devices.shape
    sizes = DP_SIZES[n_dp]
    split = Mesh(mesh.devices.reshape(*sizes, n_feat), (*DP, "feat"))
    return jax.shard_map(
        functools.partial(shards, sizes=sizes),
        mesh=split,
        in_specs=(P(DP, None), P(None, "feat"), P(DP, "feat"), P(DP), P(None, DP)),
        out_specs=(P(DP, "feat"), P(DP, "feat")),
        check_vma=False,
    )
```

```python
import functools

import jax
import jax.numpy as jnp
from jax import lax
from jax.experimental import pallas as pl
from jax.experimental.pallas import tpu as pltpu
from jax.sharding import Mesh, PartitionSpec as P

STEPS = 3
EPSILON = 1e-06
TEMPER = 50.0
MARGIN = 0.01
LOSS_SCALE = 1024.0

DP_SIZES = {64: (4, 8, 2), 8: (2, 2, 2)}
DP = ("z", "x", "yh")
LANES = 128
f32 = jnp.float32
bf16 = jnp.bfloat16
HIGHEST = lax.Precision.HIGHEST


def dot(left, right, contract, precision=None):
    return lax.dot_general(
        left, right, ((contract[:1], contract[1:]), ((), ())),
        preferred_element_type=f32, precision=precision,
    )


def passed_along(array, by):
    peers = lax.axis_size(DP)
    return lax.ppermute(array, DP, [(i, (i + by) % peers) for i in range(peers)])


def band_kernel(parts, ids, tiles, coefs):
    peers = tiles.shape[0]
    rows = parts.shape[1]
    band = ids.shape[1]
    texts = band // STEPS
    sums = jnp.sum(parts[...], 0)
    tail = sums[:, 2 * band :]
    proj_sq = jnp.concatenate([tail[s : s + 1] for s in range(STEPS)], 1)
    teach_sq = jnp.concatenate([tail[STEPS + s : STEPS + s + 1] for s in range(STEPS)], 1)
    cross = tail[2 * STEPS : 2 * STEPS + 1]
    inv_proj = lax.rsqrt(proj_sq + EPSILON)
    inv_teach = lax.rsqrt(teach_sq + EPSILON)
    both = inv_proj[:, :texts] * inv_teach[:, :texts]
    cosine = cross * both
    row_id = lax.broadcasted_iota(jnp.int32, (rows, band), 0)
    anchor = (ids[0:1, :] == row_id).astype(f32)
    own = (ids[3:4, :] == row_id).astype(f32)
    row_proj = jnp.sum(own * inv_proj, 1, keepdims=True)
    row_teach = jnp.sum(own * inv_teach, 1, keepdims=True)
    sim = sums[:, :band] * (row_proj * inv_proj)
    teach = sums[:, band : 2 * band] * (row_teach * inv_teach)
    col_id = lax.broadcasted_iota(jnp.int32, (band, band), 0)
    pick = (col_id == ids[1:2, :]).astype(f32) - (col_id == ids[2:3, :]).astype(f32)
    gap_s = jnp.sum(dot(sim, anchor, (0, 0), HIGHEST) * pick, 0, keepdims=True)
    gap_t = jnp.sum(dot(teach, anchor, (0, 0), HIGHEST) * pick, 0, keepdims=True)
    weight = jnp.tanh(TEMPER * gap_t)
    slope = -weight * jax.nn.sigmoid(TEMPER * (MARGIN - weight * gap_s))
    grad = 2.0 * (sim - teach) + dot(anchor * slope, pick, (1, 1), HIGHEST)
    product = grad * sim
    along = jnp.sum(product, 1, keepdims=True)
    inner = jnp.sum(product + along * own, 0, keepdims=True) * (inv_proj * inv_proj)
    high = inner.astype(bf16).astype(f32)
    low = inner - high
    tail_id = lax.broadcasted_iota(jnp.int32, (rows, texts), 0)
    extra = jnp.zeros((rows, texts), f32)
    for s in range(STEPS):
        piece = slice(s * texts, (s + 1) * texts)
        extra = jnp.where(tail_id == 2 * s, high[:, piece], extra)
        extra = jnp.where(tail_id == 2 * s + 1, low[:, piece], extra)
    tile = jnp.concatenate([grad * (row_proj * inv_proj), extra], 1).astype(bf16)
    for peer in range(peers):
        tiles[peer] = tile
    coefs[...] = jnp.concatenate(
        [cosine * inv_proj[:, :texts] * inv_proj[:, :texts], both, jnp.zeros((6, texts), f32)], 0
    )


def grad_kernel(gathered, coefs, proj_band, teacher, regrouped, rows_grad, grad_w):
    band = proj_band.shape[0]
    texts = band // STEPS
    gathered = gathered[...]
    tile = gathered[:, :, :band].reshape(texts, band)
    tail = jnp.sum(gathered[:, :, band:].astype(f32), 0)
    along = [
        tail[2 * s : 2 * s + 1] + tail[2 * s + 1 : 2 * s + 2] for s in range(STEPS)
    ]
    diagonal = lax.broadcasted_iota(jnp.int32, (texts, texts), 0) == lax.broadcasted_iota(
        jnp.int32, (texts, texts), 1
    )

    def upright(values):
        return jnp.sum(jnp.where(diagonal, values, 0.0), 1, keepdims=True)

    for s in range(STEPS):
        piece = slice(s * texts, (s + 1) * texts)
        lone = proj_band[piece, :].astype(f32)
        scale = -along[s]
        if s == 0:
            scale = scale + coefs[0:1, :]
        terms = dot(tile[:, piece], proj_band[0:texts, :], (0, 0)) + upright(scale) * lone
        if s == 0:
            terms = terms + dot(tile, proj_band[...], (1, 0))
            terms = terms - upright(coefs[1:2, :]) * teacher[...].astype(f32)
        rows_grad[piece, :] = (LOSS_SCALE * terms).astype(bf16)
    grad_w[...] = dot(regrouped[...], rows_grad[...], (1, 0)).astype(bf16)


def by_x(sizes, features):
    z_size, x_size, yh_size = sizes
    share = features // (z_size * x_size)
    out = lax.broadcasted_iota(jnp.int32, (features, features), 0)
    place, offset = out // share, out % share
    source = (place % z_size * x_size + place // z_size) * share + offset
    return (lax.broadcasted_iota(jnp.int32, out.shape, 1) == source).astype(bf16)


def shards(student, proj_weight, teacher, anchors, pairs, *, sizes):
    z_size, x_size, yh_size = sizes
    n_dp = z_size * x_size * yh_size
    n_feat = lax.axis_size("feat")
    texts, features = student.shape
    width = teacher.shape[1]
    band = STEPS * texts
    rows = texts // n_feat
    share = features // n_dp
    padded = -(-share // 16) * 16
    feat = lax.axis_index("feat")

    packed = jnp.concatenate([teacher, student], 1)
    near = passed_along(packed, -1)
    far = passed_along(packed, -2)

    projected = dot(student, proj_weight, (1, 0))
    teacher_wide = teacher.astype(f32)

    student_rest = jnp.concatenate([near[:, width:], far[:, width:]], 0)
    rest = dot(student_rest, proj_weight, (1, 0))
    near_teach, far_teach = near[:, :width], far[:, :width]
    proj_own = projected.astype(bf16)
    proj_rest = rest.astype(bf16)
    proj_band = jnp.concatenate([proj_own, proj_rest], 0)
    near_wide, far_wide = near_teach.astype(f32), far_teach.astype(f32)
    norms = jnp.concatenate(
        [
            jnp.sum(projected * projected, 1)[None],
            jnp.sum(rest * rest, 1).reshape(STEPS - 1, texts),
            jnp.sum(teacher_wide * teacher_wide, 1)[None],
            jnp.sum(near_wide * near_wide, 1)[None],
            jnp.sum(far_wide * far_wide, 1)[None],
            jnp.sum(projected * teacher_wide, 1)[None],
            jnp.zeros((rows - 2 * STEPS - 1, texts), f32),
        ],
        0,
    )
    parts = jnp.concatenate(
        [
            dot(proj_own, proj_own, (1, 1)),
            dot(proj_own, proj_rest, (1, 1)),
            dot(teacher, teacher, (1, 1)),
            dot(teacher, near_teach, (1, 1)),
            dot(teacher, far_teach, (1, 1)),
        ],
        1,
    ).reshape(n_feat, rows, 2 * band)
    parts = jnp.concatenate(
        [parts, jnp.broadcast_to(norms[None], (n_feat, rows, texts))], 2
    )
    parts = lax.all_to_all(parts, "feat", 0, 0)
    ids = jnp.concatenate(
        [
            anchors[None] - feat * rows,
            pairs,
            lax.broadcasted_iota(jnp.int32, (1, band), 1) - feat * rows,
            jnp.zeros((4, band), jnp.int32),
        ],
        0,
    )
    tiles, coefs = pl.pallas_call(
        band_kernel,
        out_shape=(
            jax.ShapeDtypeStruct((n_feat, rows, band + texts), bf16),
            jax.ShapeDtypeStruct((8, texts), f32),
        ),
        cost_estimate=pl.CostEstimate(flops=10**8, bytes_accessed=10**6, transcendentals=1000),
        name="band",
    )(parts, ids)
    gathered = lax.all_to_all(tiles, "feat", 0, 0)

    student_band = jnp.concatenate([student, student_rest], 0)
    regrouped = dot(by_x(sizes, features), student_band, (1, 1)).astype(bf16)
    rows_grad, grad_w = pl.pallas_call(
        grad_kernel,
        out_shape=(
            jax.ShapeDtypeStruct((band, width), bf16),
            jax.ShapeDtypeStruct((features, width), bf16),
        ),
        compiler_params=pltpu.CompilerParams(vmem_limit_bytes=32 * 2**20),
        cost_estimate=pl.CostEstimate(flops=10**9, bytes_accessed=4 * 10**6, transcendentals=0),
        name="grad",
    )(gathered, coefs, proj_band, teacher, regrouped)

    grad_w = lax.all_to_all(
        grad_w.reshape(x_size, features // x_size, width), "x", 0, 0
    ).reshape(features, width)
    zy = z_size * yh_size
    row_out = lax.broadcasted_iota(jnp.int32, (zy * padded, features), 0)
    row_in = lax.broadcasted_iota(jnp.int32, (zy * padded, features), 1) % (zy * share)
    add_rows = (
        (row_out // padded == row_in // share) & (row_out % padded == row_in % share)
    ).astype(bf16)
    grad_w = dot(add_rows, grad_w, (1, 0)).astype(bf16)
    grad_w = lax.all_to_all(grad_w.reshape(zy, padded, width), ("z", "yh"), 0, 0)
    grad_w = jnp.sum(grad_w.astype(f32), 0)[:share]

    back = dot(proj_weight, rows_grad, (1, 1)).astype(bf16)
    back = lax.all_to_all(back.reshape(n_feat, features // n_feat, band), "feat", 0, 0)
    back = jnp.sum(back.astype(f32), 0)
    grad_student = back[:, :texts]
    for s in range(1, STEPS):
        grad_student = grad_student + passed_along(back[:, s * texts : (s + 1) * texts], s)
    return (grad_w, grad_student.T)


def solution(mesh):
    n_dp, n_feat = mesh.devices.shape
    sizes = DP_SIZES[n_dp]
    split = Mesh(mesh.devices.reshape(*sizes, n_feat), (*DP, "feat"))
    return jax.shard_map(
        functools.partial(shards, sizes=sizes),
        mesh=split,
        in_specs=(P(DP, None), P(None, "feat"), P(DP, "feat"), P(DP), P(None, DP)),
        out_specs=(P(DP, "feat"), P(DP, "feat")),
        check_vma=False,
    )
```

```python
import functools

import jax
import jax.numpy as jnp
from jax import lax
from jax.experimental import pallas as pl
from jax.experimental.pallas import tpu as pltpu
from jax.sharding import Mesh, PartitionSpec as P

STEPS = 3
EPSILON = 1e-06
TEMPER = 50.0
MARGIN = 0.01
LOSS_SCALE = 1024.0

DP_SIZES = {64: (4, 8, 2), 8: (2, 2, 2)}
DP = ("z", "x", "yh")
LANES = 128
f32 = jnp.float32
bf16 = jnp.bfloat16
HIGHEST = lax.Precision.HIGHEST


def dot(left, right, contract, precision=None):
    return lax.dot_general(
        left, right, ((contract[:1], contract[1:]), ((), ())),
        preferred_element_type=f32, precision=precision,
    )


def passed_along(array, by):
    peers = lax.axis_size(DP)
    return lax.ppermute(array, DP, [(i, (i + by) % peers) for i in range(peers)])


def band_kernel(parts, sim_raw, norms, ids, tiles):
    peers = tiles.shape[0]
    rows, band = sim_raw.shape
    texts = band // STEPS
    inv_proj = lax.rsqrt(norms[0:1, :] + EPSILON)
    inv_teach = lax.rsqrt(norms[1:2, :] + EPSILON)
    row_id = lax.broadcasted_iota(jnp.int32, (rows, band), 0)
    anchor = (ids[0:1, :] == row_id).astype(f32)
    own = (ids[3:4, :] == row_id).astype(f32)
    row_proj = jnp.sum(own * inv_proj, 1, keepdims=True)
    row_teach = jnp.sum(own * inv_teach, 1, keepdims=True)
    sim = sim_raw[...] * (row_proj * inv_proj)
    teach = jnp.sum(parts[...], 0) * (row_teach * inv_teach)
    col_id = lax.broadcasted_iota(jnp.int32, (band, band), 0)
    pick = (col_id == ids[1:2, :]).astype(f32) - (col_id == ids[2:3, :]).astype(f32)
    gap_s = jnp.sum(dot(sim, anchor, (0, 0), HIGHEST) * pick, 0, keepdims=True)
    gap_t = jnp.sum(dot(teach, anchor, (0, 0), HIGHEST) * pick, 0, keepdims=True)
    weight = jnp.tanh(TEMPER * gap_t)
    slope = -weight * jax.nn.sigmoid(TEMPER * (MARGIN - weight * gap_s))
    grad = 2.0 * (sim - teach) + dot(anchor * slope, pick, (1, 1), HIGHEST)
    product = grad * sim
    along = jnp.sum(product, 1, keepdims=True)
    inner = jnp.sum(product + along * own, 0, keepdims=True) * (inv_proj * inv_proj)
    high = inner.astype(bf16).astype(f32)
    low = inner - high
    tail_id = lax.broadcasted_iota(jnp.int32, (rows, texts), 0)
    extra = jnp.zeros((rows, texts), f32)
    for s in range(STEPS):
        piece = slice(s * texts, (s + 1) * texts)
        extra = jnp.where(tail_id == 2 * s, high[:, piece], extra)
        extra = jnp.where(tail_id == 2 * s + 1, low[:, piece], extra)
    tile = jnp.concatenate([grad * (row_proj * inv_proj), extra], 1).astype(bf16)
    for peer in range(peers):
        tiles[peer] = tile


def grad_kernel(gathered, norms, proj_band, teacher, regrouped, rows_grad, grad_w):
    band = proj_band.shape[0]
    texts = band // STEPS
    gathered = gathered[...]
    tile = gathered[:, :, :band].reshape(texts, band)
    tail = jnp.sum(gathered[:, :, band:].astype(f32), 0)
    along = [
        tail[2 * s : 2 * s + 1] + tail[2 * s + 1 : 2 * s + 2] for s in range(STEPS)
    ]
    inv_proj = lax.rsqrt(norms[0:1, :texts] + EPSILON)
    inv_teach = lax.rsqrt(norms[1:2, :texts] + EPSILON)
    both = inv_proj * inv_teach
    cosine = norms[2:3, :texts] * both
    diagonal = lax.broadcasted_iota(jnp.int32, (texts, texts), 0) == lax.broadcasted_iota(
        jnp.int32, (texts, texts), 1
    )

    def upright(values):
        return jnp.sum(jnp.where(diagonal, values, 0.0), 1, keepdims=True)

    for s in range(STEPS):
        piece = slice(s * texts, (s + 1) * texts)
        lone = proj_band[piece, :].astype(f32)
        scale = -along[s]
        if s == 0:
            scale = scale + cosine * inv_proj * inv_proj
        terms = dot(tile[:, piece], proj_band[0:texts, :], (0, 0)) + upright(scale) * lone
        if s == 0:
            terms = terms + dot(tile, proj_band[...], (1, 0))
            terms = terms - upright(both) * teacher[...].astype(f32)
        rows_grad[piece, :] = (LOSS_SCALE * terms).astype(bf16)
    grad_w[...] = dot(regrouped[...], rows_grad[...], (1, 0)).astype(bf16)


def by_x(sizes, features):
    z_size, x_size, yh_size = sizes
    share = features // (z_size * x_size)
    out = lax.broadcasted_iota(jnp.int32, (features, features), 0)
    place, offset = out // share, out % share
    source = (place % z_size * x_size + place // z_size) * share + offset
    return (lax.broadcasted_iota(jnp.int32, out.shape, 1) == source).astype(bf16)


def shards(student, proj_weight, teacher, anchors, pairs, *, sizes):
    z_size, x_size, yh_size = sizes
    n_dp = z_size * x_size * yh_size
    n_feat = lax.axis_size("feat")
    texts, features = student.shape
    width = teacher.shape[1]
    band = STEPS * texts
    rows = texts // n_feat
    share = features // n_dp
    padded = -(-share // 16) * 16
    feat = lax.axis_index("feat")

    near_teach = passed_along(teacher, -1)
    far_teach = passed_along(teacher, -2)
    near_student = passed_along(student, -1)
    far_student = passed_along(student, -2)

    projected = dot(student, proj_weight, (1, 0))
    teacher_wide = teacher.astype(f32)
    proj_own = projected.astype(bf16)
    own_sums = jnp.concatenate(
        [
            jnp.sum(projected * projected, 1)[None],
            jnp.sum(teacher_wide * teacher_wide, 1)[None],
            jnp.sum(projected * teacher_wide, 1)[None],
            jnp.zeros((rows - 3, texts), f32),
        ],
        0,
    )
    through = dot(proj_own, proj_weight, (1, 1)).reshape(n_feat, rows, features)
    through = jnp.concatenate(
        [through, jnp.broadcast_to(own_sums[None], (n_feat, rows, texts))], 2
    )
    through = jnp.sum(lax.all_to_all(through, "feat", 0, 0), 0)
    own_norms = through[:8, features:]
    norms = jnp.concatenate(
        [own_norms, passed_along(own_norms, -1), passed_along(own_norms, -2)], 1
    )

    parts = jnp.concatenate(
        [
            dot(teacher, teacher, (1, 1)),
            dot(teacher, near_teach, (1, 1)),
            dot(teacher, far_teach, (1, 1)),
        ],
        1,
    )
    parts = lax.all_to_all(parts.reshape(n_feat, rows, band), "feat", 0, 0)
    student_band = jnp.concatenate([student, near_student, far_student], 0)
    sim_raw = dot(through[:, :features], student_band.astype(f32), (1, 1), HIGHEST)
    proj_rest = dot(student_band[texts:], proj_weight, (1, 0)).astype(bf16)
    proj_band = jnp.concatenate([proj_own, proj_rest], 0)
    ids = jnp.concatenate(
        [
            anchors[None] - feat * rows,
            pairs,
            lax.broadcasted_iota(jnp.int32, (1, band), 1) - feat * rows,
            jnp.zeros((4, band), jnp.int32),
        ],
        0,
    )
    tiles = pl.pallas_call(
        band_kernel,
        out_shape=jax.ShapeDtypeStruct((n_feat, rows, band + texts), bf16),
        cost_estimate=pl.CostEstimate(flops=10**8, bytes_accessed=10**6, transcendentals=1000),
        name="band",
    )(parts, sim_raw, norms, ids)
    gathered = lax.all_to_all(tiles, "feat", 0, 0)

    regrouped = dot(by_x(sizes, features), student_band, (1, 1)).astype(bf16)
    rows_grad, grad_w = pl.pallas_call(
        grad_kernel,
        out_shape=(
            jax.ShapeDtypeStruct((band, width), bf16),
            jax.ShapeDtypeStruct((features, width), bf16),
        ),
        compiler_params=pltpu.CompilerParams(vmem_limit_bytes=32 * 2**20),
        cost_estimate=pl.CostEstimate(flops=10**9, bytes_accessed=4 * 10**6, transcendentals=0),
        name="grad",
    )(gathered, norms, proj_band, teacher, regrouped)

    grad_w = lax.all_to_all(
        grad_w.reshape(x_size, features // x_size, width), "x", 0, 0
    ).reshape(features, width)
    zy = z_size * yh_size
    row_out = lax.broadcasted_iota(jnp.int32, (zy * padded, features), 0)
    row_in = lax.broadcasted_iota(jnp.int32, (zy * padded, features), 1) % (zy * share)
    add_rows = lax.optimization_barrier(
        ((row_out // padded == row_in // share) & (row_out % padded == row_in % share)).astype(bf16)
    )
    grad_w = dot(add_rows, grad_w, (1, 0)).astype(bf16)
    grad_w = lax.all_to_all(grad_w.reshape(zy, padded, width), ("z", "yh"), 0, 0)
    grad_w = jnp.sum(grad_w.astype(f32), 0)[:share]

    bits = n_feat.bit_length() - 1
    halves = proj_weight.reshape(n_feat // 2, 2, features // n_feat, width)

    def half(array, which, axis):
        return lax.dynamic_index_in_dim(array, which, axis, keepdims=False)

    def half_back(which):
        weight = half(halves, which, 1).reshape(features // 2, width)
        return dot(weight, rows_grad, (1, 1)).reshape(n_feat // 2, features // n_feat, band)

    def swapped(array, bit):
        perm = [(i, i ^ (1 << bit)) for i in range(n_feat)]
        return lax.ppermute(array.astype(bf16), "feat", perm).astype(f32)

    mine = feat & 1
    back = swapped(half_back(1 - mine), 0)
    back = half_back(mine) + back
    for bit in range(1, bits):
        back = back.reshape(-1, 2, features // n_feat, band)
        mine = (feat >> bit) & 1
        back = half(back, mine, 1) + swapped(half(back, 1 - mine, 1), bit)
    back = back.reshape(features // n_feat, band)
    grad_student = back[:, :texts]
    for s in range(1, STEPS):
        grad_student = grad_student + passed_along(back[:, s * texts : (s + 1) * texts], s)
    return (grad_w, grad_student.T)


def solution(mesh):
    n_dp, n_feat = mesh.devices.shape
    sizes = DP_SIZES[n_dp]
    split = Mesh(mesh.devices.reshape(*sizes, n_feat), (*DP, "feat"))
    return jax.shard_map(
        functools.partial(shards, sizes=sizes),
        mesh=split,
        in_specs=(P(DP, None), P(None, "feat"), P(DP, "feat"), P(DP), P(None, DP)),
        out_specs=(P(DP, "feat"), P(DP, "feat")),
        check_vma=False,
    )
```

```python
import functools

import jax
import jax.numpy as jnp
from jax import lax
from jax.experimental import pallas as pl
from jax.experimental.pallas import tpu as pltpu
from jax.sharding import Mesh, PartitionSpec as P

STEPS = 3
EPSILON = 1e-06
TEMPER = 50.0
MARGIN = 0.01
LOSS_SCALE = 1024.0

DP_SIZES = {64: (4, 8, 2), 8: (2, 2, 2)}
DP = ("z", "x", "yh")
LANES = 128
f32 = jnp.float32
bf16 = jnp.bfloat16


def dot(left, right, contract, precision=None):
    return lax.dot_general(
        left, right, ((contract[:1], contract[1:]), ((), ())),
        preferred_element_type=f32, precision=precision,
    )


def passed_along(array, by):
    peers = lax.axis_size(DP)
    return lax.ppermute(array, DP, [(i, (i + by) % peers) for i in range(peers)])


def exact_parts(values):
    high = values.astype(bf16)
    rest = values - high.astype(f32)
    middle = rest.astype(bf16)
    low = (rest - middle.astype(f32)).astype(bf16)
    return jnp.concatenate([high, middle, low], 0)


def diagonal(size):
    return lax.broadcasted_iota(jnp.int32, (size, size), 0) == lax.broadcasted_iota(
        jnp.int32, (size, size), 1
    )


def row_sums(values):
    sums = jnp.sum(values, 1, keepdims=True)
    return jnp.sum(jnp.where(diagonal(values.shape[0]), sums, 0.0), 0, keepdims=True)


def upright(values):
    return jnp.sum(jnp.where(diagonal(values.shape[1]), values, 0.0), 1, keepdims=True)


def lay_out(payload, tiles, sums):
    peers, rows, _ = payload.shape
    for t, tile in enumerate(tiles):
        texts = tile.shape[1]
        payload[:, :, t * texts : (t + 1) * texts] = tile.reshape(peers, rows, texts)
    tail = jnp.concatenate(sums + [jnp.zeros((rows - len(sums), texts), f32)], 0)
    for peer in range(peers):
        payload[peer, :, len(tiles) * texts :] = tail


def far_kernel(student, weight, teacher, far_student, far_teacher, payload, proj_own, proj_far):
    own = dot(student[...], weight[...], (1, 0))
    far = dot(far_student[...], weight[...], (1, 0))
    proj_own[...] = own.astype(bf16)
    proj_far[...] = far.astype(bf16)
    own_wide = teacher[...].astype(f32)
    far_wide = far_teacher[...].astype(f32)
    lay_out(
        payload,
        [
            dot(proj_own[...], proj_own[...], (1, 1)),
            dot(proj_own[...], proj_far[...], (1, 1)),
            dot(teacher[...], teacher[...], (1, 1)),
            dot(teacher[...], far_teacher[...], (1, 1)),
        ],
        [
            row_sums(own * own),
            row_sums(far * far),
            row_sums(own_wide * own_wide),
            row_sums(far_wide * far_wide),
            row_sums(own * own_wide),
        ],
    )


def near_kernel(proj_own, weight, teacher, near_student, near_teacher, payload, proj_near):
    near = dot(near_student[...], weight[...], (1, 0))
    proj_near[...] = near.astype(bf16)
    wide = near_teacher[...].astype(f32)
    lay_out(
        payload,
        [
            dot(proj_own[...], proj_near[...], (1, 1)),
            dot(teacher[...], near_teacher[...], (1, 1)),
        ],
        [row_sums(near * near), row_sums(wide * wide)],
    )


def band_kernel(far_parts, near_parts, ids, tiles, norms):
    peers = tiles.shape[0]
    rows = far_parts.shape[1]
    band = ids.shape[1]
    texts = band // STEPS
    far = jnp.sum(far_parts[...], 0)
    near = jnp.sum(near_parts[...], 0)

    def part(array, t):
        return array[:, t * texts : (t + 1) * texts]

    far_tail, near_tail = part(far, 4), part(near, 2)
    proj_sq = jnp.concatenate([far_tail[0:1], near_tail[0:1], far_tail[1:2]], 1)
    teach_sq = jnp.concatenate([far_tail[2:3], near_tail[1:2], far_tail[3:4]], 1)
    cross = far_tail[4:5]
    norms[...] = jnp.concatenate(
        [proj_sq[:, :texts], teach_sq[:, :texts], cross, jnp.zeros((5, texts), f32)], 0
    )
    inv_proj = lax.rsqrt(proj_sq + EPSILON)
    inv_teach = lax.rsqrt(teach_sq + EPSILON)
    row_id = lax.broadcasted_iota(jnp.int32, (rows, band), 0)
    anchor = (ids[0:1, :] == row_id).astype(f32)
    own = (ids[3:4, :] == row_id).astype(f32)
    row_proj = jnp.sum(own * inv_proj, 1, keepdims=True)
    row_teach = jnp.sum(own * inv_teach, 1, keepdims=True)
    sim = jnp.concatenate([part(far, 0), part(near, 0), part(far, 1)], 1) * (row_proj * inv_proj)
    teach = jnp.concatenate([part(far, 2), part(near, 1), part(far, 3)], 1) * (
        row_teach * inv_teach
    )
    col_id = lax.broadcasted_iota(jnp.int32, (band, band), 0)
    pick = (col_id == ids[1:2, :]).astype(f32) - (col_id == ids[2:3, :]).astype(f32)
    anchor_thrice = jnp.concatenate([anchor, anchor, anchor], 0).astype(bf16)
    gap_s = jnp.sum(dot(exact_parts(sim), anchor_thrice, (0, 0)) * pick, 0, keepdims=True)
    gap_t = jnp.sum(dot(exact_parts(teach), anchor_thrice, (0, 0)) * pick, 0, keepdims=True)
    weight = jnp.tanh(TEMPER * gap_t)
    slope = -weight * jax.nn.sigmoid(TEMPER * (MARGIN - weight * gap_s))
    added = dot(exact_parts(anchor * slope), pick.astype(bf16), (1, 1))
    grad = 2.0 * (sim - teach) + (
        added[:rows] + added[rows : 2 * rows] + added[2 * rows :]
    )
    product = grad * sim
    along = jnp.sum(product, 1, keepdims=True)
    inner = jnp.sum(product + along * own, 0, keepdims=True) * (inv_proj * inv_proj)
    high = inner.astype(bf16).astype(f32)
    low = inner - high
    tail_id = lax.broadcasted_iota(jnp.int32, (rows, texts), 0)
    extra = jnp.zeros((rows, texts), f32)
    for s in range(STEPS):
        extra = jnp.where(tail_id == 2 * s, part(high, s), extra)
        extra = jnp.where(tail_id == 2 * s + 1, part(low, s), extra)
    tile = jnp.concatenate([grad * (row_proj * inv_proj), extra], 1).astype(bf16)
    for peer in range(peers):
        tiles[peer] = tile


def grad_kernel(gathered, norms, own, near, far, teacher, regrouped, rows_grad, grad_w):
    texts = own.shape[0]
    band = STEPS * texts
    gathered = gathered[...]
    tile = gathered[:, :, :band].reshape(texts, band)
    tail = jnp.sum(gathered[:, :, band:].astype(f32), 0)
    inv_proj = lax.rsqrt(norms[0:1, :] + EPSILON)
    inv_teach = lax.rsqrt(norms[1:2, :] + EPSILON)
    both = inv_proj * inv_teach
    cosine = norms[2:3, :] * both
    for s, partner in enumerate((own, near, far)):
        piece = slice(s * texts, (s + 1) * texts)
        scale = -(tail[2 * s : 2 * s + 1] + tail[2 * s + 1 : 2 * s + 2])
        if s == 0:
            scale = scale + cosine * inv_proj * inv_proj
        terms = dot(tile[:, piece], own[...], (0, 0)) + upright(scale) * partner[...].astype(f32)
        if s == 0:
            for other, mate in enumerate((own, near, far)):
                terms = terms + dot(
                    tile[:, other * texts : (other + 1) * texts], mate[...], (1, 0)
                )
            terms = terms - upright(both) * teacher[...].astype(f32)
        rows_grad[piece, :] = (LOSS_SCALE * terms).astype(bf16)
    grad_w[...] = dot(regrouped[...], rows_grad[...], (1, 0)).astype(bf16)


def add_kernel(received, out):
    blocks, padded, _ = out.shape
    total = jnp.sum(received[...].astype(f32), 0)
    share = total.shape[0] // blocks
    fill = jnp.zeros((padded - share, total.shape[1]), f32)
    for block in range(blocks):
        piece = total[block * share : (block + 1) * share]
        out[block] = jnp.concatenate([piece, fill], 0).astype(bf16)


def by_x(sizes, features):
    z_size, x_size, yh_size = sizes
    share = features // (z_size * x_size)
    out = lax.broadcasted_iota(jnp.int32, (features, features), 0)
    place, offset = out // share, out % share
    source = (place % z_size * x_size + place // z_size) * share + offset
    return (lax.broadcasted_iota(jnp.int32, out.shape, 1) == source).astype(bf16)


def shards(student, proj_weight, teacher, anchors, pairs, *, sizes):
    z_size, x_size, yh_size = sizes
    n_dp = z_size * x_size * yh_size
    n_feat = lax.axis_size("feat")
    texts, features = student.shape
    width = teacher.shape[1]
    band = STEPS * texts
    rows = texts // n_feat
    share = features // n_dp
    padded = -(-share // 16) * 16
    feat = lax.axis_index("feat")

    near_student = passed_along(student, -1)
    near_teacher = passed_along(teacher, -1)
    far_student = passed_along(student, -2)
    far_teacher = passed_along(teacher, -2)

    def cost(flops):
        return pl.CostEstimate(flops=flops, bytes_accessed=3 * 10**6, transcendentals=0)

    rows_type = jax.ShapeDtypeStruct((texts, width), bf16)
    far_parts, proj_own, proj_far = pl.pallas_call(
        far_kernel,
        out_shape=(jax.ShapeDtypeStruct((n_feat, rows, 5 * texts), f32), rows_type, rows_type),
        compiler_params=pltpu.CompilerParams(vmem_limit_bytes=16 * 2**20),
        cost_estimate=cost(6 * 10**8),
        name="far",
    )(student, proj_weight, teacher, far_student, far_teacher)
    far_parts = lax.all_to_all(far_parts, "feat", 0, 0)
    near_parts, proj_near = pl.pallas_call(
        near_kernel,
        out_shape=(jax.ShapeDtypeStruct((n_feat, rows, 3 * texts), f32), rows_type),
        compiler_params=pltpu.CompilerParams(vmem_limit_bytes=16 * 2**20),
        cost_estimate=cost(3 * 10**8),
        name="near",
    )(proj_own, proj_weight, teacher, near_student, near_teacher)
    near_parts = lax.all_to_all(near_parts, "feat", 0, 0)

    ids = jnp.concatenate(
        [
            anchors[None] - feat * rows,
            pairs,
            lax.broadcasted_iota(jnp.int32, (1, band), 1) - feat * rows,
            jnp.zeros((4, band), jnp.int32),
        ],
        0,
    )
    tiles, norms = pl.pallas_call(
        band_kernel,
        out_shape=(
            jax.ShapeDtypeStruct((n_feat, rows, band + texts), bf16),
            jax.ShapeDtypeStruct((8, texts), f32),
        ),
        cost_estimate=cost(10**8),
        name="band",
    )(far_parts, near_parts, ids)
    gathered = lax.all_to_all(tiles, "feat", 0, 0)

    student_band = jnp.concatenate([student, near_student, far_student], 0)
    regrouped = dot(by_x(sizes, features), student_band, (1, 1)).astype(bf16)
    rows_grad, grad_w = pl.pallas_call(
        grad_kernel,
        out_shape=(
            jax.ShapeDtypeStruct((band, width), bf16),
            jax.ShapeDtypeStruct((features, width), bf16),
        ),
        compiler_params=pltpu.CompilerParams(vmem_limit_bytes=16 * 2**20),
        cost_estimate=cost(10**9),
        name="grad",
    )(gathered, norms, proj_own, proj_near, proj_far, teacher, regrouped)

    zy = z_size * yh_size
    grad_w = lax.all_to_all(grad_w.reshape(x_size, features // x_size, width), "x", 0, 0)
    columns = min(width, 256)
    grad_w = pl.pallas_call(
        add_kernel,
        grid=(width // columns,),
        in_specs=[pl.BlockSpec((x_size, features // x_size, columns), lambda i: (0, 0, i))],
        out_specs=pl.BlockSpec((zy, padded, columns), lambda i: (0, 0, i)),
        out_shape=jax.ShapeDtypeStruct((zy, padded, width), bf16),
        cost_estimate=cost(10**6),
        name="add",
    )(grad_w)
    grad_w = lax.all_to_all(grad_w, ("z", "yh"), 0, 0)
    grad_w = jnp.sum(grad_w.astype(f32), 0)[:share]

    halves = proj_weight.reshape(n_feat // 2, 2, features // n_feat, width)

    def half_back(core):
        weight = lax.dynamic_index_in_dim(halves, core, 1, keepdims=False)
        weight = weight.reshape(features // 2, width)
        back = dot(weight, rows_grad, (1, 1))
        return back.reshape(n_feat // 2, features // n_feat, band)

    def swapped(array, mask):
        perm = [(i, i ^ mask) for i in range(n_feat)]
        return lax.ppermute(array.astype(bf16), "feat", perm).astype(f32)

    core = feat & 1
    back = swapped(half_back(1 - core), 1)
    back = half_back(core) + back
    chip = feat >> 1
    mine = lax.dynamic_index_in_dim(back, chip, 0, keepdims=False)
    for other in range(1, n_feat // 2):
        theirs = lax.dynamic_index_in_dim(back, chip ^ other, 0, keepdims=False)
        mine = mine + swapped(theirs, 2 * other)
    grad_student = mine[:, :texts]
    for s in range(1, STEPS):
        grad_student = grad_student + passed_along(mine[:, s * texts : (s + 1) * texts], s)
    return (grad_w, grad_student.T)


def solution(mesh):
    n_dp, n_feat = mesh.devices.shape
    sizes = DP_SIZES[n_dp]
    split = Mesh(mesh.devices.reshape(*sizes, n_feat), (*DP, "feat"))
    return jax.shard_map(
        functools.partial(shards, sizes=sizes),
        mesh=split,
        in_specs=(P(DP, None), P(None, "feat"), P(DP, "feat"), P(DP), P(None, DP)),
        out_specs=(P(DP, "feat"), P(DP, "feat")),
        check_vma=False,
    )
```

```python
import functools

import jax
import jax.numpy as jnp
from jax import lax
from jax.experimental import pallas as pl
from jax.experimental.pallas import tpu as pltpu
from jax.sharding import Mesh, PartitionSpec as P

STEPS = 3
EPSILON = 1e-06
TEMPER = 50.0
MARGIN = 0.01
LOSS_SCALE = 1024.0

DP_SIZES = {64: (4, 8, 2), 8: (2, 2, 2)}
DP = ("z", "x", "yh")
LANES = 128
f32 = jnp.float32
bf16 = jnp.bfloat16


def dot(left, right, contract, precision=None):
    return lax.dot_general(
        left, right, ((contract[:1], contract[1:]), ((), ())),
        preferred_element_type=f32, precision=precision,
    )


def passed_along(array, by):
    peers = lax.axis_size(DP)
    return lax.ppermute(array, DP, [(i, (i + by) % peers) for i in range(peers)])


def exact_parts(values):
    high = values.astype(bf16)
    rest = values - high.astype(f32)
    middle = rest.astype(bf16)
    low = (rest - middle.astype(f32)).astype(bf16)
    return jnp.concatenate([high, middle, low], 0)


def diagonal(size):
    return lax.broadcasted_iota(jnp.int32, (size, size), 0) == lax.broadcasted_iota(
        jnp.int32, (size, size), 1
    )


def row_sums(values):
    sums = jnp.sum(values, 1, keepdims=True)
    return jnp.sum(jnp.where(diagonal(values.shape[0]), sums, 0.0), 0, keepdims=True)


def upright(values):
    return jnp.sum(jnp.where(diagonal(values.shape[1]), values, 0.0), 1, keepdims=True)


def own_kernel(student, weight, weight_rows, teacher, through, proj_own, tiles, sums):
    peers, height, _ = through.shape
    texts = student.shape[0]
    own = dot(student[...], weight[...], (1, 0))
    proj_own[...] = own.astype(bf16)
    wide = teacher[...].astype(f32)
    tiles[:, :texts] = dot(proj_own[...], proj_own[...], (1, 1))
    tiles[:, texts:] = dot(teacher[...], teacher[...], (1, 1))
    sums[...] = jnp.concatenate(
        [row_sums(own * own), row_sums(wide * wide), row_sums(own * wide), jnp.zeros((5, texts), f32)],
        0,
    )
    for t, other in enumerate((weight_rows, teacher)):
        product = dot(weight[...], other[...], (1, 1)).astype(bf16)
        through[:, :, t * LANES : (t + 1) * LANES] = product.reshape(peers, height, LANES)


def tile_kernel(
    proj_own, weight, teacher, tiles, sums, near_student, far_student, near_teacher, far_teacher,
    payload, proj_near, proj_far,
):
    peers, rows, _ = payload.shape
    texts = proj_own.shape[0]
    tail = [sums[0:1, :], sums[1:2, :], sums[2:3, :]]

    def lay_out(t, tile):
        payload[:, :, t * texts : (t + 1) * texts] = tile.reshape(peers, rows, texts)

    lay_out(0, tiles[:, :texts])
    lay_out(STEPS, tiles[:, texts:])
    for s, rows_in, mates_in, proj in (
        (1, near_student, near_teacher, proj_near),
        (2, far_student, far_teacher, proj_far),
    ):
        other = dot(rows_in[...], weight[...], (1, 0))
        proj[...] = other.astype(bf16)
        wide = mates_in[...].astype(f32)
        tail = tail + [row_sums(other * other), row_sums(wide * wide)]
        lay_out(s, dot(proj_own[...], proj[...], (1, 1)))
        lay_out(STEPS + s, dot(teacher[...], mates_in[...], (1, 1)))
    tail = jnp.concatenate(tail + [jnp.zeros((rows - len(tail), texts), f32)], 0)
    for peer in range(peers):
        payload[peer, :, 2 * STEPS * texts :] = tail


def band_kernel(parts, ids, tiles, norms):
    peers = tiles.shape[0]
    rows = parts.shape[1]
    band = ids.shape[1]
    texts = band // STEPS
    sums = jnp.sum(parts[...], 0)

    def part(array, t):
        return array[:, t * texts : (t + 1) * texts]

    tail = part(sums, 2 * STEPS)
    norms[...] = tail[:8]
    proj_sq = jnp.concatenate([tail[0:1], tail[3:4], tail[5:6]], 1)
    teach_sq = jnp.concatenate([tail[1:2], tail[4:5], tail[6:7]], 1)
    inv_proj = lax.rsqrt(proj_sq + EPSILON)
    inv_teach = lax.rsqrt(teach_sq + EPSILON)
    row_id = lax.broadcasted_iota(jnp.int32, (rows, band), 0)
    anchor = (ids[0:1, :] == row_id).astype(f32)
    own = (ids[3:4, :] == row_id).astype(f32)
    row_proj = jnp.sum(own * inv_proj, 1, keepdims=True)
    row_teach = jnp.sum(own * inv_teach, 1, keepdims=True)
    sim = sums[:, :band] * (row_proj * inv_proj)
    teach = sums[:, band : 2 * band] * (row_teach * inv_teach)
    col_id = lax.broadcasted_iota(jnp.int32, (band, band), 0)
    pick = (col_id == ids[1:2, :]).astype(f32) - (col_id == ids[2:3, :]).astype(f32)
    anchor_thrice = jnp.concatenate([anchor, anchor, anchor], 0).astype(bf16)
    gap_s = jnp.sum(dot(exact_parts(sim), anchor_thrice, (0, 0)) * pick, 0, keepdims=True)
    gap_t = jnp.sum(dot(exact_parts(teach), anchor_thrice, (0, 0)) * pick, 0, keepdims=True)
    weight = jnp.tanh(TEMPER * gap_t)
    slope = -weight * jax.nn.sigmoid(TEMPER * (MARGIN - weight * gap_s))
    added = dot(exact_parts(anchor * slope), pick.astype(bf16), (1, 1))
    grad = 2.0 * (sim - teach) + (
        added[:rows] + added[rows : 2 * rows] + added[2 * rows :]
    )
    product = grad * sim
    along = jnp.sum(product, 1, keepdims=True)
    inner = jnp.sum(product + along * own, 0, keepdims=True) * (inv_proj * inv_proj)
    high = inner.astype(bf16).astype(f32)
    low = inner - high
    tail_id = lax.broadcasted_iota(jnp.int32, (rows, texts), 0)
    extra = jnp.zeros((rows, texts), f32)
    for s in range(STEPS):
        extra = jnp.where(tail_id == 2 * s, part(high, s), extra)
        extra = jnp.where(tail_id == 2 * s + 1, part(low, s), extra)
    tile = jnp.concatenate([grad * (row_proj * inv_proj), extra], 1).astype(bf16)
    for peer in range(peers):
        tiles[peer] = tile


def spread(gathered, norms, rows):
    own = rows[0]
    texts = own.shape[0]
    band = STEPS * texts
    gathered = gathered[...]
    tile = gathered[:, :, :band].reshape(texts, band)
    tail = jnp.sum(gathered[:, :, band:].astype(f32), 0)
    inv_proj = lax.rsqrt(norms[0:1, :] + EPSILON)
    inv_teach = lax.rsqrt(norms[1:2, :] + EPSILON)
    both = inv_proj * inv_teach
    cosine = norms[2:3, :] * both
    terms = []
    for s, partner in enumerate(rows):
        scale = -(tail[2 * s : 2 * s + 1] + tail[2 * s + 1 : 2 * s + 2])
        if s == 0:
            scale = scale + cosine * inv_proj * inv_proj
        tile_s = tile[:, s * texts : (s + 1) * texts]
        terms.append(dot(tile_s, own[...], (0, 0)) + upright(scale) * partner[...].astype(f32))
        terms[0] = terms[0] + dot(tile_s, partner[...], (1, 0))
    return terms, both


def grad_kernel(gathered, norms, own, near, far, teacher, regrouped, rows_grad, grad_w):
    texts = own.shape[0]
    terms, both = spread(gathered, norms, (own, near, far))
    terms[0] = terms[0] - upright(both) * teacher[...].astype(f32)
    for s in range(STEPS):
        rows_grad[s * texts : (s + 1) * texts, :] = (LOSS_SCALE * terms[s]).astype(bf16)
    grad_w[...] = dot(regrouped[...], rows_grad[...], (1, 0)).astype(bf16)


def student_kernel(gathered, norms, own, near, far, gram, teacher_back, out_own, out_near, out_far):
    terms, both = spread(gathered, norms, (own, near, far))
    groups = own.shape[1] // LANES
    table = jnp.concatenate([gram[g] for g in range(groups)], 1)
    for s, out in enumerate((out_own, out_near, out_far)):
        product = dot(table, terms[s].astype(bf16), (1, 1))
        if s == 0:
            product = product - both * teacher_back[...]
        out[...] = LOSS_SCALE * product


def add_kernel(received, out):
    blocks, padded, _ = out.shape
    total = jnp.sum(received[...].astype(f32), 0)
    share = total.shape[0] // blocks
    fill = jnp.zeros((padded - share, total.shape[1]), f32)
    for block in range(blocks):
        piece = total[block * share : (block + 1) * share]
        out[block] = jnp.concatenate([piece, fill], 0).astype(bf16)


def by_x(sizes, features):
    z_size, x_size, yh_size = sizes
    share = features // (z_size * x_size)
    out = lax.broadcasted_iota(jnp.int32, (features, features), 0)
    place, offset = out // share, out % share
    source = (place % z_size * x_size + place // z_size) * share + offset
    return (lax.broadcasted_iota(jnp.int32, out.shape, 1) == source).astype(bf16)


def shards(student, proj_weight, teacher, anchors, pairs, *, sizes):
    z_size, x_size, yh_size = sizes
    n_dp = z_size * x_size * yh_size
    n_feat = lax.axis_size("feat")
    texts, features = student.shape
    width = teacher.shape[1]
    band = STEPS * texts
    rows = texts // n_feat
    share = features // n_dp
    padded = -(-share // 16) * 16
    feat = lax.axis_index("feat")

    near_student = passed_along(student, -1)
    near_teacher = passed_along(teacher, -1)

    def cost(flops):
        return pl.CostEstimate(flops=flops, bytes_accessed=3 * 10**6, transcendentals=0)

    params = pltpu.CompilerParams(vmem_limit_bytes=16 * 2**20)
    rows_type = jax.ShapeDtypeStruct((texts, width), bf16)

    groups = features // LANES
    height = features // n_feat
    row_start = jnp.minimum(lax.axis_index("x"), groups - 1) * LANES
    weight_rows = lax.dynamic_slice(proj_weight, (row_start, 0), (LANES, width))
    through, proj_own, own_tiles, own_sums = pl.pallas_call(
        own_kernel,
        out_shape=(
            jax.ShapeDtypeStruct((n_feat, height, 2 * LANES), bf16),
            rows_type,
            jax.ShapeDtypeStruct((texts, 2 * texts), f32),
            jax.ShapeDtypeStruct((8, texts), f32),
        ),
        compiler_params=params,
        cost_estimate=cost(6 * 10**8),
        name="own",
    )(student, proj_weight, weight_rows, teacher)
    far_rows = lax.optimization_barrier((student, teacher, proj_own))
    far_student = passed_along(far_rows[0], -2)
    far_teacher = passed_along(far_rows[1], -2)
    through = jnp.sum(lax.all_to_all(through, "feat", 0, 0).astype(f32), 0)
    teacher_back = through[:, LANES:]
    gram = through[:, :LANES].astype(bf16)
    gram = lax.all_to_all(jnp.broadcast_to(gram[None], (x_size, height, LANES)), "x", 0, 0)

    parts, proj_near, proj_far = pl.pallas_call(
        tile_kernel,
        out_shape=(
            jax.ShapeDtypeStruct((n_feat, rows, (2 * STEPS + 1) * texts), f32),
            rows_type,
            rows_type,
        ),
        compiler_params=params,
        cost_estimate=cost(6 * 10**8),
        name="tile",
    )(
        proj_own, proj_weight, teacher, own_tiles, own_sums,
        near_student, far_student, near_teacher, far_teacher,
    )
    parts = lax.all_to_all(parts, "feat", 0, 0)

    ids = jnp.concatenate(
        [
            anchors[None] - feat * rows,
            pairs,
            lax.broadcasted_iota(jnp.int32, (1, band), 1) - feat * rows,
            jnp.zeros((4, band), jnp.int32),
        ],
        0,
    )
    tiles, norms = pl.pallas_call(
        band_kernel,
        out_shape=(
            jax.ShapeDtypeStruct((n_feat, rows, band + texts), bf16),
            jax.ShapeDtypeStruct((8, texts), f32),
        ),
        cost_estimate=cost(10**8),
        name="band",
    )(parts, ids)
    gathered = lax.all_to_all(tiles, "feat", 0, 0)

    student_band = jnp.concatenate([student, near_student, far_student], 0)
    regrouped = dot(by_x(sizes, features), student_band, (1, 1)).astype(bf16)
    _, grad_w = pl.pallas_call(
        grad_kernel,
        out_shape=(
            jax.ShapeDtypeStruct((band, width), bf16),
            jax.ShapeDtypeStruct((features, width), bf16),
        ),
        compiler_params=params,
        cost_estimate=cost(10**9),
        name="grad",
    )(gathered, norms, proj_own, proj_near, proj_far, teacher, regrouped)

    zy = z_size * yh_size
    grad_w = lax.all_to_all(grad_w.reshape(x_size, features // x_size, width), "x", 0, 0)
    grad_w = pl.pallas_call(
        add_kernel,
        grid=(z_size,),
        in_specs=[pl.BlockSpec((x_size, yh_size * share, width), lambda i: (0, i, 0))],
        out_specs=pl.BlockSpec((yh_size, padded, width), lambda i: (i, 0, 0)),
        out_shape=jax.ShapeDtypeStruct((zy, padded, width), bf16),
        cost_estimate=cost(10**6),
        name="add",
    )(grad_w)
    grad_w = lax.all_to_all(grad_w, ("z", "yh"), 0, 0)
    grad_w = jnp.sum(grad_w.astype(f32), 0)[:share]

    columns_type = jax.ShapeDtypeStruct((height, texts), f32)
    own, near, far = pl.pallas_call(
        student_kernel,
        out_shape=(columns_type,) * STEPS,
        compiler_params=params,
        cost_estimate=cost(4 * 10**8),
        name="student",
    )(gathered, norms, student, near_student, far_student, gram, teacher_back)
    grad_student = own + passed_along(near, 1) + passed_along(far, 2)
    return (grad_w, grad_student.T)


def solution(mesh):
    n_dp, n_feat = mesh.devices.shape
    sizes = DP_SIZES[n_dp]
    split = Mesh(mesh.devices.reshape(*sizes, n_feat), (*DP, "feat"))
    return jax.shard_map(
        functools.partial(shards, sizes=sizes),
        mesh=split,
        in_specs=(P(DP, None), P(None, "feat"), P(DP, "feat"), P(DP), P(None, DP)),
        out_specs=(P(DP, "feat"), P(DP, "feat")),
        check_vma=False,
    )
```

```python
import functools

import jax
import jax.numpy as jnp
from jax import lax
from jax.experimental import pallas as pl
from jax.experimental.pallas import tpu as pltpu
from jax.sharding import Mesh, PartitionSpec as P

STEPS = 3
EPSILON = 1e-06
TEMPER = 50.0
MARGIN = 0.01
LOSS_SCALE = 1024.0

DP_SIZES = {64: (4, 8, 2), 8: (2, 2, 2)}
DP = ("z", "x", "yh")
LANES = 128
f32 = jnp.float32
bf16 = jnp.bfloat16


def dot(left, right, contract):
    return lax.dot_general(
        left, right, ((contract[:1], contract[1:]), ((), ())),
        preferred_element_type=f32,
    )


def passed_along(array, by):
    peers = lax.axis_size(DP)
    return lax.ppermute(array, DP, [(i, (i + by) % peers) for i in range(peers)])


def exact_parts(values):
    high = values.astype(bf16)
    rest = values - high.astype(f32)
    middle = rest.astype(bf16)
    low = (rest - middle.astype(f32)).astype(bf16)
    return jnp.concatenate([high, middle, low], 0)


def diagonal(size):
    return lax.broadcasted_iota(jnp.int32, (size, size), 0) == lax.broadcasted_iota(
        jnp.int32, (size, size), 1
    )


def row_sums(values):
    sums = jnp.sum(values, 1, keepdims=True)
    return jnp.sum(jnp.where(diagonal(values.shape[0]), sums, 0.0), 0, keepdims=True)


def upright(values):
    return jnp.sum(jnp.where(diagonal(values.shape[1]), values, 0.0), 1, keepdims=True)


def own_kernel(student, weight, weight_rows, teacher, through, proj_own, tiles, sums):
    peers, height, _ = through.shape
    texts = student.shape[0]
    own = dot(student[...], weight[...], (1, 0))
    proj_own[...] = own.astype(bf16)
    wide = teacher[...].astype(f32)
    tiles[:, :texts] = dot(proj_own[...], proj_own[...], (1, 1))
    tiles[:, texts:] = dot(teacher[...], teacher[...], (1, 1))
    sums[...] = jnp.concatenate(
        [row_sums(own * own), row_sums(wide * wide), row_sums(own * wide), jnp.zeros((5, texts), f32)],
        0,
    )
    for t, other in enumerate((weight_rows, teacher)):
        product = dot(weight[...], other[...], (1, 1)).astype(bf16)
        through[:, :, t * LANES : (t + 1) * LANES] = product.reshape(peers, height, LANES)


def tile_kernel(
    proj_own, weight, teacher, tiles, sums, near_student, far_student, near_teacher, far_teacher,
    payload, proj_near, proj_far,
):
    peers, rows, _ = payload.shape
    texts = proj_own.shape[0]
    tail = [sums[0:1, :], sums[1:2, :], sums[2:3, :]]

    def lay_out(t, tile):
        payload[:, :, t * texts : (t + 1) * texts] = tile.reshape(peers, rows, texts)

    lay_out(0, tiles[:, :texts])
    lay_out(STEPS, tiles[:, texts:])
    for s, rows_in, mates_in, proj in (
        (1, near_student, near_teacher, proj_near),
        (2, far_student, far_teacher, proj_far),
    ):
        other = dot(rows_in[...], weight[...], (1, 0))
        proj[...] = other.astype(bf16)
        wide = mates_in[...].astype(f32)
        tail = tail + [row_sums(other * other), row_sums(wide * wide)]
        lay_out(s, dot(proj_own[...], proj[...], (1, 1)))
        lay_out(STEPS + s, dot(teacher[...], mates_in[...], (1, 1)))
    tail = jnp.concatenate(tail + [jnp.zeros((rows - len(tail), texts), f32)], 0)
    for peer in range(peers):
        payload[peer, :, 2 * STEPS * texts :] = tail


def band_kernel(parts, ids, tiles, norms):
    peers = tiles.shape[0]
    rows = parts.shape[1]
    band = ids.shape[1]
    texts = band // STEPS
    sums = jnp.sum(parts[...], 0)

    def part(array, t):
        return array[:, t * texts : (t + 1) * texts]

    tail = part(sums, 2 * STEPS)
    norms[...] = tail[:8]
    proj_sq = jnp.concatenate([tail[0:1], tail[3:4], tail[5:6]], 1)
    teach_sq = jnp.concatenate([tail[1:2], tail[4:5], tail[6:7]], 1)
    inv_proj = lax.rsqrt(proj_sq + EPSILON)
    inv_teach = lax.rsqrt(teach_sq + EPSILON)
    row_id = lax.broadcasted_iota(jnp.int32, (rows, band), 0)
    anchor = (ids[0:1, :] == row_id).astype(f32)
    own = (ids[3:4, :] == row_id).astype(f32)
    row_proj = jnp.sum(own * inv_proj, 1, keepdims=True)
    row_teach = jnp.sum(own * inv_teach, 1, keepdims=True)
    sim = sums[:, :band] * (row_proj * inv_proj)
    teach = sums[:, band : 2 * band] * (row_teach * inv_teach)
    col_id = lax.broadcasted_iota(jnp.int32, (band, band), 0)
    pick = (col_id == ids[1:2, :]).astype(f32) - (col_id == ids[2:3, :]).astype(f32)
    anchor_thrice = jnp.concatenate([anchor, anchor, anchor], 0).astype(bf16)
    gap_s = jnp.sum(dot(exact_parts(sim), anchor_thrice, (0, 0)) * pick, 0, keepdims=True)
    gap_t = jnp.sum(dot(exact_parts(teach), anchor_thrice, (0, 0)) * pick, 0, keepdims=True)
    weight = jnp.tanh(TEMPER * gap_t)
    slope = -weight * jax.nn.sigmoid(TEMPER * (MARGIN - weight * gap_s))
    added = dot(exact_parts(anchor * slope), pick.astype(bf16), (1, 1))
    grad = 2.0 * (sim - teach) + (
        added[:rows] + added[rows : 2 * rows] + added[2 * rows :]
    )
    product = grad * sim
    along = jnp.sum(product, 1, keepdims=True)
    inner = jnp.sum(product + along * own, 0, keepdims=True) * (inv_proj * inv_proj)
    high = inner.astype(bf16).astype(f32)
    low = inner - high
    tail_id = lax.broadcasted_iota(jnp.int32, (rows, texts), 0)
    extra = jnp.zeros((rows, texts), f32)
    for s in range(STEPS):
        extra = jnp.where(tail_id == 2 * s, part(high, s), extra)
        extra = jnp.where(tail_id == 2 * s + 1, part(low, s), extra)
    tile = jnp.concatenate([grad * (row_proj * inv_proj), extra], 1).astype(bf16)
    for peer in range(peers):
        tiles[peer] = tile


def spread(gathered, norms, rows):
    own = rows[0]
    texts = own.shape[0]
    band = STEPS * texts
    gathered = gathered[...]
    tile = gathered[:, :, :band].reshape(texts, band)
    tail = jnp.sum(gathered[:, :, band:].astype(f32), 0)
    inv_proj = lax.rsqrt(norms[0:1, :] + EPSILON)
    inv_teach = lax.rsqrt(norms[1:2, :] + EPSILON)
    both = inv_proj * inv_teach
    cosine = norms[2:3, :] * both
    terms = []
    for s, partner in enumerate(rows):
        scale = -(tail[2 * s : 2 * s + 1] + tail[2 * s + 1 : 2 * s + 2])
        if s == 0:
            scale = scale + cosine * inv_proj * inv_proj
        tile_s = tile[:, s * texts : (s + 1) * texts]
        terms.append(dot(tile_s, own[...], (0, 0)) + upright(scale) * partner[...].astype(f32))
        terms[0] = terms[0] + dot(tile_s, partner[...], (1, 0))
    return terms, both


def grad_kernel(
    sizes, gathered, norms, own, near, far, teacher, student, near_student, far_student, grad_w
):
    z_size, x_size, _ = sizes
    terms, both = spread(gathered, norms, (own, near, far))
    terms[0] = terms[0] - upright(both) * teacher[...].astype(f32)
    total = 0.0
    for term, rows in zip(terms, (student, near_student, far_student)):
        total = total + dot(rows[...], (LOSS_SCALE * term).astype(bf16), (0, 0))
    step = total.shape[0] // (z_size * x_size)
    starts = [(z * x_size + x) * step for x in range(x_size) for z in range(z_size)]
    grad_w[...] = jnp.concatenate([total[r : r + step] for r in starts], 0).astype(bf16)


def student_kernel(gathered, norms, own, near, far, gram, teacher_back, out_own, out_near, out_far):
    terms, both = spread(gathered, norms, (own, near, far))
    groups = own.shape[1] // LANES
    table = jnp.concatenate([gram[g] for g in range(groups)], 1)
    for s, out in enumerate((out_own, out_near, out_far)):
        product = dot(table, terms[s].astype(bf16), (1, 1))
        if s == 0:
            product = product - both * teacher_back[...]
        out[...] = LOSS_SCALE * product


def add_kernel(select, received, out, held, sems):
    peers = received.shape[0]
    copies = [
        pltpu.make_async_copy(received.at[p], held.at[p], sems.at[p]) for p in range(peers)
    ]
    for copy in copies:
        copy.start()
    total = 0.0
    for peer, copy in enumerate(copies):
        copy.wait()
        total = total + dot(select[...], held[peer], (1, 0))
    out[...] = total.astype(bf16)


def shards(student, proj_weight, teacher, anchors, pairs, *, sizes):
    z_size, x_size, yh_size = sizes
    n_dp = z_size * x_size * yh_size
    n_feat = lax.axis_size("feat")
    texts, features = student.shape
    width = teacher.shape[1]
    band = STEPS * texts
    rows = texts // n_feat
    share = features // n_dp
    padded = -(-share // 16) * 16
    feat = lax.axis_index("feat")

    near_student = passed_along(student, -1)
    near_teacher = passed_along(teacher, -1)
    far_student = passed_along(student, -2)
    far_teacher = passed_along(teacher, -2)

    def cost(flops):
        return pl.CostEstimate(flops=flops, bytes_accessed=3 * 10**6, transcendentals=0)

    params = pltpu.CompilerParams(vmem_limit_bytes=16 * 2**20)
    rows_type = jax.ShapeDtypeStruct((texts, width), bf16)

    groups = features // LANES
    height = features // n_feat
    row_start = jnp.minimum(lax.axis_index("x"), groups - 1) * LANES
    weight_rows = lax.dynamic_slice(proj_weight, (row_start, 0), (LANES, width))
    through, proj_own, own_tiles, own_sums = pl.pallas_call(
        own_kernel,
        out_shape=(
            jax.ShapeDtypeStruct((n_feat, height, 2 * LANES), bf16),
            rows_type,
            jax.ShapeDtypeStruct((texts, 2 * texts), f32),
            jax.ShapeDtypeStruct((8, texts), f32),
        ),
        compiler_params=params,
        cost_estimate=cost(6 * 10**8),
        name="own",
    )(student, proj_weight, weight_rows, teacher)

    parts, proj_near, proj_far = pl.pallas_call(
        tile_kernel,
        out_shape=(
            jax.ShapeDtypeStruct((n_feat, rows, (2 * STEPS + 1) * texts), f32),
            rows_type,
            rows_type,
        ),
        compiler_params=params,
        cost_estimate=cost(6 * 10**8),
        name="tile",
    )(
        proj_own, proj_weight, teacher, own_tiles, own_sums,
        near_student, far_student, near_teacher, far_teacher,
    )
    through, parts = lax.optimization_barrier((through, parts))
    parts = lax.all_to_all(parts, "feat", 0, 0)
    through = lax.psum_scatter(through, "feat", scatter_dimension=0, tiled=False)

    ids = jnp.concatenate(
        [
            anchors[None] - feat * rows,
            pairs,
            lax.broadcasted_iota(jnp.int32, (1, band), 1) - feat * rows,
            jnp.zeros((4, band), jnp.int32),
        ],
        0,
    )
    tiles, norms = pl.pallas_call(
        band_kernel,
        out_shape=(
            jax.ShapeDtypeStruct((n_feat, rows, band + texts), bf16),
            jax.ShapeDtypeStruct((8, texts), f32),
        ),
        cost_estimate=cost(10**8),
        name="band",
    )(parts, ids)
    gathered = lax.all_to_all(tiles, "feat", 0, 0)

    grad_w = pl.pallas_call(
        functools.partial(grad_kernel, sizes),
        out_shape=jax.ShapeDtypeStruct((features, width), bf16),
        compiler_params=params,
        cost_estimate=cost(10**9),
        name="grad",
    )(
        gathered, norms, proj_own, proj_near, proj_far, teacher, student, near_student, far_student
    )
    grad_w, through = lax.optimization_barrier((grad_w, through))

    zy = z_size * yh_size
    grad_w = lax.all_to_all(grad_w.reshape(x_size, features // x_size, width), "x", 0, 0)
    row_out = lax.broadcasted_iota(jnp.int32, (zy * padded, zy * share), 0)
    row_in = lax.broadcasted_iota(jnp.int32, row_out.shape, 1)
    select = (row_out // padded == row_in // share) & (row_out % padded == row_in % share)
    grad_w = pl.pallas_call(
        add_kernel,
        in_specs=[pl.BlockSpec(memory_space=pltpu.VMEM), pl.BlockSpec(memory_space=pl.ANY)],
        out_shape=jax.ShapeDtypeStruct((zy * padded, width), bf16),
        scratch_shapes=[
            pltpu.VMEM((x_size, features // x_size, width), bf16),
            pltpu.SemaphoreType.DMA((x_size,)),
        ],
        compiler_params=params,
        cost_estimate=cost(10**8),
        name="add",
    )(lax.optimization_barrier(select.astype(bf16)), grad_w)
    grad_w = lax.all_to_all(grad_w.reshape(zy, padded, width), ("z", "yh"), 0, 0)
    grad_w = jnp.sum(grad_w.astype(f32), 0)[:share]

    gram = lax.all_gather(through[:, :LANES], "x")
    teacher_back = through[:, LANES:].astype(f32)
    columns_type = jax.ShapeDtypeStruct((height, texts), f32)
    own, near, far = pl.pallas_call(
        student_kernel,
        out_shape=(columns_type,) * STEPS,
        compiler_params=params,
        cost_estimate=cost(4 * 10**8),
        name="student",
    )(gathered, norms, student, near_student, far_student, gram, teacher_back)
    grad_student = own + passed_along(near, 1) + passed_along(far, 2)
    return (grad_w, grad_student.T)


def solution(mesh):
    n_dp, n_feat = mesh.devices.shape
    sizes = DP_SIZES[n_dp]
    split = Mesh(mesh.devices.reshape(*sizes, n_feat), (*DP, "feat"))
    return jax.shard_map(
        functools.partial(shards, sizes=sizes),
        mesh=split,
        in_specs=(P(DP, None), P(None, "feat"), P(DP, "feat"), P(DP), P(None, DP)),
        out_specs=(P(DP, "feat"), P(DP, "feat")),
        check_vma=False,
    )
```

```python
import functools

import jax
import jax.numpy as jnp
from jax import lax
from jax.experimental import pallas as pl
from jax.experimental.pallas import tpu as pltpu
from jax.sharding import Mesh, PartitionSpec as P

STEPS = 3
EPSILON = 1e-06
TEMPER = 50.0
MARGIN = 0.01
LOSS_SCALE = 1024.0

DP_SIZES = {64: (4, 8, 2), 8: (2, 2, 2)}
DP = ("z", "x", "yh")
LANES = 128
f32 = jnp.float32
bf16 = jnp.bfloat16


def dot(left, right, contract):
    return lax.dot_general(
        left, right, ((contract[:1], contract[1:]), ((), ())),
        preferred_element_type=f32,
    )


def passed_along(array, by):
    peers = lax.axis_size(DP)
    return lax.ppermute(array, DP, [(i, (i + by) % peers) for i in range(peers)])


def exact_parts(values):
    high = values.astype(bf16)
    rest = values - high.astype(f32)
    middle = rest.astype(bf16)
    low = (rest - middle.astype(f32)).astype(bf16)
    return jnp.concatenate([high, middle, low], 0)


def diagonal(size):
    return lax.broadcasted_iota(jnp.int32, (size, size), 0) == lax.broadcasted_iota(
        jnp.int32, (size, size), 1
    )


def row_sums(values):
    sums = jnp.sum(values, 1, keepdims=True)
    return jnp.sum(jnp.where(diagonal(values.shape[0]), sums, 0.0), 0, keepdims=True)


def upright(values):
    return jnp.sum(jnp.where(diagonal(values.shape[1]), values, 0.0), 1, keepdims=True)


def own_kernel(student, weight, teacher, proj_own, tiles, sums):
    texts = student.shape[0]
    own = dot(student[...], weight[...], (1, 0))
    proj_own[...] = own.astype(bf16)
    wide = teacher[...].astype(f32)
    tiles[:, :texts] = dot(proj_own[...], proj_own[...], (1, 1))
    tiles[:, texts:] = dot(teacher[...], teacher[...], (1, 1))
    sums[...] = jnp.concatenate(
        [row_sums(own * own), row_sums(wide * wide), row_sums(own * wide), jnp.zeros((5, texts), f32)],
        0,
    )


def tile_kernel(
    proj_own, weight, teacher, tiles, sums, near_student, far_student, near_teacher, far_teacher,
    payload, proj_near, proj_far,
):
    peers, rows, _ = payload.shape
    texts = proj_own.shape[0]
    tail = [sums[0:1, :], sums[1:2, :], sums[2:3, :]]

    def lay_out(t, tile):
        payload[:, :, t * texts : (t + 1) * texts] = tile.reshape(peers, rows, texts)

    lay_out(0, tiles[:, :texts])
    lay_out(STEPS, tiles[:, texts:])
    for s, rows_in, mates_in, proj in (
        (1, near_student, near_teacher, proj_near),
        (2, far_student, far_teacher, proj_far),
    ):
        other = dot(rows_in[...], weight[...], (1, 0))
        proj[...] = other.astype(bf16)
        wide = mates_in[...].astype(f32)
        tail = tail + [row_sums(other * other), row_sums(wide * wide)]
        lay_out(s, dot(proj_own[...], proj[...], (1, 1)))
        lay_out(STEPS + s, dot(teacher[...], mates_in[...], (1, 1)))
    tail = jnp.concatenate(tail + [jnp.zeros((rows - len(tail), texts), f32)], 0)
    for peer in range(peers):
        payload[peer, :, 2 * STEPS * texts :] = tail


def band_kernel(parts, ids, tiles, norms):
    peers = tiles.shape[0]
    rows = parts.shape[1]
    band = ids.shape[1]
    texts = band // STEPS
    sums = jnp.sum(parts[...], 0)

    def part(array, t):
        return array[:, t * texts : (t + 1) * texts]

    tail = part(sums, 2 * STEPS)
    norms[...] = tail[:8]
    proj_sq = jnp.concatenate([tail[0:1], tail[3:4], tail[5:6]], 1)
    teach_sq = jnp.concatenate([tail[1:2], tail[4:5], tail[6:7]], 1)
    inv_proj = lax.rsqrt(proj_sq + EPSILON)
    inv_teach = lax.rsqrt(teach_sq + EPSILON)
    row_id = lax.broadcasted_iota(jnp.int32, (rows, band), 0)
    anchor = (ids[0:1, :] == row_id).astype(f32)
    own = (ids[3:4, :] == row_id).astype(f32)
    row_proj = jnp.sum(own * inv_proj, 1, keepdims=True)
    row_teach = jnp.sum(own * inv_teach, 1, keepdims=True)
    sim = sums[:, :band] * (row_proj * inv_proj)
    teach = sums[:, band : 2 * band] * (row_teach * inv_teach)
    col_id = lax.broadcasted_iota(jnp.int32, (band, band), 0)
    pick = (col_id == ids[1:2, :]).astype(f32) - (col_id == ids[2:3, :]).astype(f32)
    anchor_thrice = jnp.concatenate([anchor, anchor, anchor], 0).astype(bf16)
    gap_s = jnp.sum(dot(exact_parts(sim), anchor_thrice, (0, 0)) * pick, 0, keepdims=True)
    gap_t = jnp.sum(dot(exact_parts(teach), anchor_thrice, (0, 0)) * pick, 0, keepdims=True)
    weight = jnp.tanh(TEMPER * gap_t)
    slope = -weight * jax.nn.sigmoid(TEMPER * (MARGIN - weight * gap_s))
    added = dot(exact_parts(anchor * slope), pick.astype(bf16), (1, 1))
    grad = 2.0 * (sim - teach) + (
        added[:rows] + added[rows : 2 * rows] + added[2 * rows :]
    )
    product = grad * sim
    along = jnp.sum(product, 1, keepdims=True)
    inner = jnp.sum(product + along * own, 0, keepdims=True) * (inv_proj * inv_proj)
    high = inner.astype(bf16).astype(f32)
    low = inner - high
    tail_id = lax.broadcasted_iota(jnp.int32, (rows, texts), 0)
    extra = jnp.zeros((rows, texts), f32)
    for s in range(STEPS):
        extra = jnp.where(tail_id == 2 * s, part(high, s), extra)
        extra = jnp.where(tail_id == 2 * s + 1, part(low, s), extra)
    tile = jnp.concatenate([grad * (row_proj * inv_proj), extra], 1).astype(bf16)
    for peer in range(peers):
        tiles[peer] = tile


def spread(gathered, norms, rows):
    own = rows[0]
    texts = own.shape[0]
    band = STEPS * texts
    gathered = gathered[...]
    tile = gathered[:, :, :band].reshape(texts, band)
    tail = jnp.sum(gathered[:, :, band:].astype(f32), 0)
    inv_proj = lax.rsqrt(norms[0:1, :] + EPSILON)
    inv_teach = lax.rsqrt(norms[1:2, :] + EPSILON)
    both = inv_proj * inv_teach
    cosine = norms[2:3, :] * both
    terms = []
    for s, partner in enumerate(rows):
        scale = -(tail[2 * s : 2 * s + 1] + tail[2 * s + 1 : 2 * s + 2])
        if s == 0:
            scale = scale + cosine * inv_proj * inv_proj
        tile_s = tile[:, s * texts : (s + 1) * texts]
        terms.append(dot(tile_s, own[...], (0, 0)) + upright(scale) * partner[...].astype(f32))
        terms[0] = terms[0] + dot(tile_s, partner[...], (1, 0))
    return terms, both


def grad_kernel(
    sizes, gathered, norms, own, near, far, teacher, student, near_student, far_student,
    rows_grad, grad_w,
):
    z_size, x_size, _ = sizes
    texts = own.shape[0]
    terms, both = spread(gathered, norms, (own, near, far))
    terms[0] = terms[0] - upright(both) * teacher[...].astype(f32)
    total = 0.0
    for s, rows in enumerate((student, near_student, far_student)):
        piece = slice(s * texts, (s + 1) * texts)
        rows_grad[piece, :] = (LOSS_SCALE * terms[s]).astype(bf16)
        total = total + dot(rows[...], rows_grad[piece, :], (0, 0))
    step = total.shape[0] // (z_size * x_size)
    starts = [(z * x_size + x) * step for x in range(x_size) for z in range(z_size)]
    grad_w[...] = jnp.concatenate([total[r : r + step] for r in starts], 0).astype(bf16)


def shards(student, proj_weight, teacher, anchors, pairs, *, sizes):
    z_size, x_size, yh_size = sizes
    n_dp = z_size * x_size * yh_size
    n_feat = lax.axis_size("feat")
    texts, features = student.shape
    width = teacher.shape[1]
    band = STEPS * texts
    rows = texts // n_feat
    share = features // n_dp
    padded = -(-share // 16) * 16
    feat = lax.axis_index("feat")

    near_student = passed_along(student, -1)
    near_teacher = passed_along(teacher, -1)
    far_student = passed_along(student, -2)
    far_teacher = passed_along(teacher, -2)

    def cost(flops):
        return pl.CostEstimate(flops=flops, bytes_accessed=3 * 10**6, transcendentals=0)

    params = pltpu.CompilerParams(vmem_limit_bytes=16 * 2**20)
    rows_type = jax.ShapeDtypeStruct((texts, width), bf16)

    proj_own, own_tiles, own_sums = pl.pallas_call(
        own_kernel,
        out_shape=(
            rows_type,
            jax.ShapeDtypeStruct((texts, 2 * texts), f32),
            jax.ShapeDtypeStruct((8, texts), f32),
        ),
        compiler_params=params,
        cost_estimate=cost(3 * 10**8),
        name="own",
    )(student, proj_weight, teacher)

    parts, proj_near, proj_far = pl.pallas_call(
        tile_kernel,
        out_shape=(
            jax.ShapeDtypeStruct((n_feat, rows, (2 * STEPS + 1) * texts), f32),
            rows_type,
            rows_type,
        ),
        compiler_params=params,
        cost_estimate=cost(6 * 10**8),
        name="tile",
    )(
        proj_own, proj_weight, teacher, own_tiles, own_sums,
        near_student, far_student, near_teacher, far_teacher,
    )
    parts = lax.all_to_all(parts, "feat", 0, 0)

    ids = jnp.concatenate(
        [
            anchors[None] - feat * rows,
            pairs,
            lax.broadcasted_iota(jnp.int32, (1, band), 1) - feat * rows,
            jnp.zeros((4, band), jnp.int32),
        ],
        0,
    )
    tiles, norms = pl.pallas_call(
        band_kernel,
        out_shape=(
            jax.ShapeDtypeStruct((n_feat, rows, band + texts), bf16),
            jax.ShapeDtypeStruct((8, texts), f32),
        ),
        cost_estimate=cost(10**8),
        name="band",
    )(parts, ids)
    gathered = lax.all_to_all(tiles, "feat", 0, 0)

    rows_grad, grad_w = pl.pallas_call(
        functools.partial(grad_kernel, sizes),
        out_shape=(
            jax.ShapeDtypeStruct((band, width), bf16),
            jax.ShapeDtypeStruct((features, width), bf16),
        ),
        compiler_params=params,
        cost_estimate=cost(10**9),
        name="grad",
    )(
        gathered, norms, proj_own, proj_near, proj_far, teacher, student, near_student, far_student
    )

    zy = z_size * yh_size
    grad_w = lax.all_to_all(
        grad_w.reshape(x_size, features // x_size, width), "x", 0, 0
    ).reshape(features, width)
    row_out = lax.broadcasted_iota(jnp.int32, (zy * padded, features), 0)
    row_in = lax.broadcasted_iota(jnp.int32, row_out.shape, 1) % (zy * share)
    select = (row_out // padded == row_in // share) & (row_out % padded == row_in % share)
    select = lax.optimization_barrier(select.astype(bf16))
    grad_w = dot(select, grad_w, (1, 0)).astype(bf16)
    grad_w = lax.all_to_all(grad_w.reshape(zy, padded, width), ("z", "yh"), 0, 0)
    grad_w = jnp.sum(grad_w.astype(f32), 0)[:share]

    height = features // n_feat
    halves = proj_weight.reshape(n_feat // 2, 2, height, width)

    def half(array, which, axis):
        return lax.dynamic_index_in_dim(array, which, axis, keepdims=False)

    def half_back(which):
        weight = half(halves, which, 1).reshape(features // 2, width)
        return dot(weight, rows_grad, (1, 1)).reshape(n_feat // 2, height, band)

    def swapped(array, bit):
        perm = [(i, i ^ (1 << bit)) for i in range(n_feat)]
        return lax.ppermute(array.astype(bf16), "feat", perm).astype(f32)

    mine = feat & 1
    back = swapped(half_back(1 - mine), 0)
    back = half_back(mine) + back
    for bit in range(1, n_feat.bit_length() - 1):
        back = back.reshape(-1, 2, height, band)
        mine = (feat >> bit) & 1
        back = half(back, mine, 1) + swapped(half(back, 1 - mine, 1), bit)
    back = back.reshape(height, band)
    grad_student = back[:, :texts]
    for s in range(1, STEPS):
        grad_student = grad_student + passed_along(back[:, s * texts : (s + 1) * texts], s)
    return (grad_w, grad_student.T)


def solution(mesh):
    n_dp, n_feat = mesh.devices.shape
    sizes = DP_SIZES[n_dp]
    split = Mesh(mesh.devices.reshape(*sizes, n_feat), (*DP, "feat"))
    return jax.shard_map(
        functools.partial(shards, sizes=sizes),
        mesh=split,
        in_specs=(P(DP, None), P(None, "feat"), P(DP, "feat"), P(DP), P(None, DP)),
        out_specs=(P(DP, "feat"), P(DP, "feat")),
        check_vma=False,
    )
```

```python
import functools

import jax
import jax.numpy as jnp
from jax import lax
from jax.experimental import pallas as pl
from jax.experimental.pallas import tpu as pltpu
from jax.sharding import Mesh, PartitionSpec as P

STEPS = 3
EPSILON = 1e-06
TEMPER = 50.0
MARGIN = 0.01
LOSS_SCALE = 1024.0

DP_SIZES = {64: (4, 8, 2), 8: (2, 2, 2)}
DP = ("z", "x", "yh")
LANES = 128
f32 = jnp.float32
bf16 = jnp.bfloat16


def dot(left, right, contract):
    return lax.dot_general(
        left, right, ((contract[:1], contract[1:]), ((), ())),
        preferred_element_type=f32,
    )


def passed_along(array, by):
    peers = lax.axis_size(DP)
    return lax.ppermute(array, DP, [(i, (i + by) % peers) for i in range(peers)])


def exact_parts(values):
    high = values.astype(bf16)
    rest = values - high.astype(f32)
    middle = rest.astype(bf16)
    low = (rest - middle.astype(f32)).astype(bf16)
    return jnp.concatenate([high, middle, low], 0)


def diagonal(size):
    return lax.broadcasted_iota(jnp.int32, (size, size), 0) == lax.broadcasted_iota(
        jnp.int32, (size, size), 1
    )


def row_sums(values):
    sums = jnp.sum(values, 1, keepdims=True)
    return jnp.sum(jnp.where(diagonal(values.shape[0]), sums, 0.0), 0, keepdims=True)


def upright(values):
    return jnp.sum(jnp.where(diagonal(values.shape[1]), values, 0.0), 1, keepdims=True)


def own_kernel(student, weight, teacher, proj_own, tiles, sums):
    texts = student.shape[0]
    own = dot(student[...], weight[...], (1, 0))
    proj_own[...] = own.astype(bf16)
    wide = teacher[...].astype(f32)
    tiles[:, :texts] = dot(proj_own[...], proj_own[...], (1, 1))
    tiles[:, texts:] = dot(teacher[...], teacher[...], (1, 1))
    sums[...] = jnp.concatenate(
        [row_sums(own * own), row_sums(wide * wide), row_sums(own * wide), jnp.zeros((5, texts), f32)],
        0,
    )


def tile_kernel(
    proj_own, weight, teacher, tiles, sums, near_student, far_student, near_teacher, far_teacher,
    payload,
):
    peers, rows, _ = payload.shape
    texts = proj_own.shape[0]
    tail = [sums[0:1, :], sums[1:2, :], sums[2:3, :]]

    def lay_out(t, tile):
        payload[:, :, t * texts : (t + 1) * texts] = tile.reshape(peers, rows, texts)

    lay_out(0, tiles[:, :texts])
    lay_out(STEPS, tiles[:, texts:])
    for s, rows_in, mates_in in (
        (1, near_student, near_teacher),
        (2, far_student, far_teacher),
    ):
        projected = dot(rows_in[...], weight[...], (1, 0))
        wide = mates_in[...].astype(f32)
        tail = tail + [row_sums(projected * projected), row_sums(wide * wide)]
        lay_out(s, dot(proj_own[...], projected.astype(bf16), (1, 1)))
        lay_out(STEPS + s, dot(teacher[...], mates_in[...], (1, 1)))
    tail = jnp.concatenate(tail + [jnp.zeros((rows - len(tail), texts), f32)], 0)
    for peer in range(peers):
        payload[peer, :, 2 * STEPS * texts :] = tail


def band_kernel(parts, ids, tiles):
    peers = tiles.shape[0]
    rows = parts.shape[1]
    band = ids.shape[1]
    texts = band // STEPS
    sums = jnp.sum(parts[...], 0)

    def part(array, t):
        return array[:, t * texts : (t + 1) * texts]

    tail = part(sums, 2 * STEPS)
    proj_sq = jnp.concatenate([tail[0:1], tail[3:4], tail[5:6]], 1)
    teach_sq = jnp.concatenate([tail[1:2], tail[4:5], tail[6:7]], 1)
    inv_proj = lax.rsqrt(proj_sq + EPSILON)
    inv_teach = lax.rsqrt(teach_sq + EPSILON)
    row_id = lax.broadcasted_iota(jnp.int32, (rows, band), 0)
    anchor = (ids[0:1, :] == row_id).astype(f32)
    own = (ids[3:4, :] == row_id).astype(f32)
    row_proj = jnp.sum(own * inv_proj, 1, keepdims=True)
    row_teach = jnp.sum(own * inv_teach, 1, keepdims=True)
    sim = sums[:, :band] * (row_proj * inv_proj)
    teach = sums[:, band : 2 * band] * (row_teach * inv_teach)
    col_id = lax.broadcasted_iota(jnp.int32, (band, band), 0)
    pick = (col_id == ids[1:2, :]).astype(f32) - (col_id == ids[2:3, :]).astype(f32)
    anchor_thrice = jnp.concatenate([anchor, anchor, anchor], 0).astype(bf16)
    gap_s = jnp.sum(dot(exact_parts(sim), anchor_thrice, (0, 0)) * pick, 0, keepdims=True)
    gap_t = jnp.sum(dot(exact_parts(teach), anchor_thrice, (0, 0)) * pick, 0, keepdims=True)
    weight = jnp.tanh(TEMPER * gap_t)
    slope = -weight * jax.nn.sigmoid(TEMPER * (MARGIN - weight * gap_s))
    added = dot(exact_parts(anchor * slope), pick.astype(bf16), (1, 1))
    grad = 2.0 * (sim - teach) + (
        added[:rows] + added[rows : 2 * rows] + added[2 * rows :]
    )
    product = grad * sim
    along = jnp.sum(product, 1, keepdims=True)
    inner = jnp.sum(product + along * own, 0, keepdims=True) * (inv_proj * inv_proj)
    both = inv_proj[:, :texts] * inv_teach[:, :texts]
    cosine = tail[2:3] * both * inv_proj[:, :texts] * inv_proj[:, :texts]
    rows_out = [
        part(inner, 0) - cosine * (1.0 / peers), part(inner, 1), part(inner, 2), both * (1.0 / peers)
    ]
    tail_id = lax.broadcasted_iota(jnp.int32, (rows, texts), 0)
    extra = jnp.zeros((rows, texts), f32)
    for r, row in enumerate(rows_out):
        high = row.astype(bf16).astype(f32)
        extra = jnp.where(tail_id == 2 * r, high, extra)
        extra = jnp.where(tail_id == 2 * r + 1, row - high, extra)
    tile = jnp.concatenate([grad * (row_proj * inv_proj), extra], 1).astype(bf16)
    for peer in range(peers):
        tiles[peer] = tile


def grad_kernel(
    sizes, gathered, weight, teacher, student, near_student, far_student,
    rows_grad, grad_w,
):
    z_size, x_size, _ = sizes
    texts = student.shape[0]
    band = STEPS * texts
    rows_in = (student, near_student, far_student)
    projected = [dot(rows[...], weight[...], (1, 0)).astype(bf16) for rows in rows_in]
    tile = gathered[:, :, :band].reshape(texts, band)
    tail = jnp.sum(gathered[:, :, band:].astype(f32), 0)
    tail = [tail[2 * r : 2 * r + 1] + tail[2 * r + 1 : 2 * r + 2] for r in range(STEPS + 1)]
    terms = []
    for s in range(STEPS):
        tile_s = tile[:, s * texts : (s + 1) * texts]
        terms.append(dot(tile_s, projected[0], (0, 0)) - upright(tail[s]) * projected[s].astype(f32))
        terms[0] = terms[0] + dot(tile_s, projected[s], (1, 0))
    terms[0] = terms[0] - upright(tail[STEPS]) * teacher[...].astype(f32)
    total = 0.0
    for s, rows in enumerate(rows_in):
        piece = slice(s * texts, (s + 1) * texts)
        rows_grad[piece, :] = (LOSS_SCALE * terms[s]).astype(bf16)
        total = total + dot(rows[...], rows_grad[piece, :], (0, 0))
    step = total.shape[0] // (z_size * x_size)
    starts = [(z * x_size + x) * step for x in range(x_size) for z in range(z_size)]
    grad_w[...] = jnp.concatenate([total[r : r + step] for r in starts], 0).astype(bf16)


def shards(student, proj_weight, teacher, anchors, pairs, *, sizes):
    z_size, x_size, yh_size = sizes
    n_dp = z_size * x_size * yh_size
    n_feat = lax.axis_size("feat")
    texts, features = student.shape
    width = teacher.shape[1]
    band = STEPS * texts
    rows = texts // n_feat
    share = features // n_dp
    padded = -(-share // 16) * 16
    feat = lax.axis_index("feat")

    near_student = passed_along(student, -1)
    near_teacher = passed_along(teacher, -1)
    far_student = passed_along(student, -2)
    far_teacher = passed_along(teacher, -2)

    def cost(flops):
        return pl.CostEstimate(flops=flops, bytes_accessed=3 * 10**6, transcendentals=0)

    params = pltpu.CompilerParams(vmem_limit_bytes=16 * 2**20)
    rows_type = jax.ShapeDtypeStruct((texts, width), bf16)

    proj_own, own_tiles, own_sums = pl.pallas_call(
        own_kernel,
        out_shape=(
            rows_type,
            jax.ShapeDtypeStruct((texts, 2 * texts), f32),
            jax.ShapeDtypeStruct((8, texts), f32),
        ),
        compiler_params=params,
        cost_estimate=cost(3 * 10**8),
        name="own",
    )(student, proj_weight, teacher)

    parts = pl.pallas_call(
        tile_kernel,
        out_shape=jax.ShapeDtypeStruct((n_feat, rows, (2 * STEPS + 1) * texts), f32),
        compiler_params=params,
        cost_estimate=cost(6 * 10**8),
        name="tile",
    )(
        proj_own, proj_weight, teacher, own_tiles, own_sums,
        near_student, far_student, near_teacher, far_teacher,
    )
    parts = lax.all_to_all(parts, "feat", 0, 0)

    ids = jnp.concatenate(
        [
            anchors[None] - feat * rows,
            pairs,
            lax.broadcasted_iota(jnp.int32, (1, band), 1) - feat * rows,
            jnp.zeros((4, band), jnp.int32),
        ],
        0,
    )
    tiles = pl.pallas_call(
        band_kernel,
        out_shape=jax.ShapeDtypeStruct((n_feat, rows, band + texts), bf16),
        cost_estimate=cost(10**8),
        name="band",
    )(parts, ids)
    gathered = lax.all_to_all(tiles, "feat", 0, 0)

    rows_grad, grad_w = pl.pallas_call(
        functools.partial(grad_kernel, sizes),
        out_shape=(
            jax.ShapeDtypeStruct((band, width), bf16),
            jax.ShapeDtypeStruct((features, width), bf16),
        ),
        compiler_params=params,
        cost_estimate=cost(10**9),
        name="grad",
    )(gathered, proj_weight, teacher, student, near_student, far_student)

    zy = z_size * yh_size
    grad_w = lax.all_to_all(
        grad_w.reshape(x_size, features // x_size, width), "x", 0, 0
    ).reshape(features, width)
    row_out = lax.broadcasted_iota(jnp.int32, (zy * padded, features), 0)
    row_in = lax.broadcasted_iota(jnp.int32, row_out.shape, 1) % (zy * share)
    select = (row_out // padded == row_in // share) & (row_out % padded == row_in % share)
    select = lax.optimization_barrier(select.astype(bf16))
    grad_w = dot(select, grad_w, (1, 0)).astype(bf16)
    grad_w = lax.all_to_all(grad_w.reshape(zy, padded, width), ("z", "yh"), 0, 0)
    grad_w = jnp.sum(grad_w.astype(f32), 0)[:share]

    height = features // n_feat
    halves = proj_weight.reshape(n_feat // 2, 2, height, width)

    def half(array, which, axis):
        return lax.dynamic_index_in_dim(array, which, axis, keepdims=False)

    def half_back(which):
        weight = half(halves, which, 1).reshape(features // 2, width)
        return dot(weight, rows_grad, (1, 1)).reshape(n_feat // 2, height, band)

    def swapped(array, bit):
        perm = [(i, i ^ (1 << bit)) for i in range(n_feat)]
        return lax.ppermute(array.astype(bf16), "feat", perm).astype(f32)

    mine = feat & 1
    back = swapped(half_back(1 - mine), 0)
    back = half_back(mine) + back
    for bit in range(1, n_feat.bit_length() - 1):
        back = back.reshape(-1, 2, height, band)
        mine = (feat >> bit) & 1
        back = half(back, mine, 1) + swapped(half(back, 1 - mine, 1), bit)
    back = back.reshape(height, band)
    grad_student = back[:, :texts]
    for s in range(1, STEPS):
        grad_student = grad_student + passed_along(back[:, s * texts : (s + 1) * texts], s)
    return (grad_w, grad_student.T)


def solution(mesh):
    n_dp, n_feat = mesh.devices.shape
    sizes = DP_SIZES[n_dp]
    split = Mesh(mesh.devices.reshape(*sizes, n_feat), (*DP, "feat"))
    return jax.shard_map(
        functools.partial(shards, sizes=sizes),
        mesh=split,
        in_specs=(P(DP, None), P(None, "feat"), P(DP, "feat"), P(DP), P(None, DP)),
        out_specs=(P(DP, "feat"), P(DP, "feat")),
        check_vma=False,
    )
```

```python
import functools

import jax
import jax.numpy as jnp
from jax import lax
from jax.experimental import pallas as pl
from jax.experimental.pallas import tpu as pltpu
from jax.sharding import Mesh, PartitionSpec as P

STEPS = 3
EPSILON = 1e-06
TEMPER = 50.0
MARGIN = 0.01
LOSS_SCALE = 1024.0

DP_SIZES = {64: (4, 8, 2), 8: (2, 2, 2)}
DP = ("z", "x", "yh")
LANES = 128
f32 = jnp.float32
bf16 = jnp.bfloat16


def dot(left, right, contract):
    return lax.dot_general(
        left, right, ((contract[:1], contract[1:]), ((), ())),
        preferred_element_type=f32,
    )


def passed_along(array, by):
    peers = lax.axis_size(DP)
    return lax.ppermute(array, DP, [(i, (i + by) % peers) for i in range(peers)])


def exact_parts(values):
    high = values.astype(bf16)
    rest = values - high.astype(f32)
    middle = rest.astype(bf16)
    low = (rest - middle.astype(f32)).astype(bf16)
    return jnp.concatenate([high, middle, low], 0)


def diagonal(size):
    return lax.broadcasted_iota(jnp.int32, (size, size), 0) == lax.broadcasted_iota(
        jnp.int32, (size, size), 1
    )


def row_sums(values):
    sums = jnp.sum(values, 1, keepdims=True)
    return jnp.sum(jnp.where(diagonal(values.shape[0]), sums, 0.0), 0, keepdims=True)


def upright(values):
    return jnp.sum(jnp.where(diagonal(values.shape[1]), values, 0.0), 1, keepdims=True)


def own_kernel(student, weight, teacher, proj_own, tiles, sums):
    texts = student.shape[0]
    own = dot(student[...], weight[...], (1, 0))
    proj_own[...] = own.astype(bf16)
    wide = teacher[...].astype(f32)
    tiles[:, :texts] = dot(proj_own[...], proj_own[...], (1, 1))
    tiles[:, texts:] = dot(teacher[...], teacher[...], (1, 1))
    sums[...] = jnp.concatenate(
        [row_sums(own * own), row_sums(wide * wide), row_sums(own * wide), jnp.zeros((5, texts), f32)],
        0,
    )


def tile_kernel(
    proj_own, weight, teacher, tiles, sums, near_student, far_student, near_teacher, far_teacher,
    payload,
):
    peers, rows, _ = payload.shape
    texts = proj_own.shape[0]
    tail = [sums[0:1, :], sums[1:2, :], sums[2:3, :]]

    def lay_out(t, tile):
        payload[:, :, t * texts : (t + 1) * texts] = tile.reshape(peers, rows, texts)

    lay_out(0, tiles[:, :texts])
    lay_out(STEPS, tiles[:, texts:])
    for s, rows_in, mates_in in (
        (1, near_student, near_teacher),
        (2, far_student, far_teacher),
    ):
        projected = dot(rows_in[...], weight[...], (1, 0))
        wide = mates_in[...].astype(f32)
        tail = tail + [row_sums(projected * projected), row_sums(wide * wide)]
        lay_out(s, dot(proj_own[...], projected.astype(bf16), (1, 1)))
        lay_out(STEPS + s, dot(teacher[...], mates_in[...], (1, 1)))
    tail = jnp.concatenate(tail + [jnp.zeros((rows - len(tail), texts), f32)], 0)
    for peer in range(peers):
        payload[peer, :, 2 * STEPS * texts :] = tail


def band_kernel(parts, ids, tiles):
    peers = tiles.shape[0]
    rows = parts.shape[1]
    band = ids.shape[1]
    texts = band // STEPS
    sums = jnp.sum(parts[...], 0)

    def part(array, t):
        return array[:, t * texts : (t + 1) * texts]

    tail = part(sums, 2 * STEPS)
    proj_sq = jnp.concatenate([tail[0:1], tail[3:4], tail[5:6]], 1)
    teach_sq = jnp.concatenate([tail[1:2], tail[4:5], tail[6:7]], 1)
    inv_proj = lax.rsqrt(proj_sq + EPSILON)
    inv_teach = lax.rsqrt(teach_sq + EPSILON)
    row_id = lax.broadcasted_iota(jnp.int32, (rows, band), 0)
    anchor = (ids[0:1, :] == row_id).astype(f32)
    own = (ids[3:4, :] == row_id).astype(f32)
    row_proj = jnp.sum(own * inv_proj, 1, keepdims=True)
    row_teach = jnp.sum(own * inv_teach, 1, keepdims=True)
    sim = sums[:, :band] * (row_proj * inv_proj)
    teach = sums[:, band : 2 * band] * (row_teach * inv_teach)
    col_id = lax.broadcasted_iota(jnp.int32, (band, band), 0)
    pick = (col_id == ids[1:2, :]).astype(f32) - (col_id == ids[2:3, :]).astype(f32)
    anchor_thrice = jnp.concatenate([anchor, anchor, anchor], 0).astype(bf16)
    gap_s = jnp.sum(dot(exact_parts(sim), anchor_thrice, (0, 0)) * pick, 0, keepdims=True)
    gap_t = jnp.sum(dot(exact_parts(teach), anchor_thrice, (0, 0)) * pick, 0, keepdims=True)
    weight = jnp.tanh(TEMPER * gap_t)
    slope = -weight * jax.nn.sigmoid(TEMPER * (MARGIN - weight * gap_s))
    added = dot(exact_parts(anchor * slope), pick.astype(bf16), (1, 1))
    grad = 2.0 * (sim - teach) + (
        added[:rows] + added[rows : 2 * rows] + added[2 * rows :]
    )
    product = grad * sim
    along = jnp.sum(product, 1, keepdims=True)
    inner = jnp.sum(product + along * own, 0, keepdims=True) * (inv_proj * inv_proj)
    both = inv_proj[:, :texts] * inv_teach[:, :texts]
    cosine = tail[2:3] * both * inv_proj[:, :texts] * inv_proj[:, :texts]
    rows_out = [
        part(inner, 0) - cosine * (1.0 / peers), part(inner, 1), part(inner, 2), both * (1.0 / peers)
    ]
    tail_id = lax.broadcasted_iota(jnp.int32, (rows, texts), 0)
    extra = jnp.zeros((rows, texts), f32)
    for r, row in enumerate(rows_out):
        high = row.astype(bf16).astype(f32)
        extra = jnp.where(tail_id == 2 * r, high, extra)
        extra = jnp.where(tail_id == 2 * r + 1, row - high, extra)
    tile = jnp.concatenate([grad * (row_proj * inv_proj), extra], 1).astype(bf16)
    for peer in range(peers):
        tiles[peer] = tile


def grad_kernel(
    sizes, gathered, weight, teacher, student, near_student, far_student,
    rows_grad, grad_w,
):
    z_size, x_size, _ = sizes
    texts = student.shape[0]
    band = STEPS * texts
    rows_in = (student, near_student, far_student)
    projected = [dot(rows[...], weight[...], (1, 0)).astype(bf16) for rows in rows_in]
    tile = gathered[:, :, :band].reshape(texts, band)
    tail = jnp.sum(gathered[:, :, band:].astype(f32), 0)
    tail = [tail[2 * r : 2 * r + 1] + tail[2 * r + 1 : 2 * r + 2] for r in range(STEPS + 1)]
    terms = []
    for s in range(STEPS):
        tile_s = tile[:, s * texts : (s + 1) * texts]
        terms.append(dot(tile_s, projected[0], (0, 0)) - upright(tail[s]) * projected[s].astype(f32))
        terms[0] = terms[0] + dot(tile_s, projected[s], (1, 0))
    terms[0] = terms[0] - upright(tail[STEPS]) * teacher[...].astype(f32)
    total = 0.0
    for s, rows in enumerate(rows_in):
        piece = slice(s * texts, (s + 1) * texts)
        rows_grad[piece, :] = (LOSS_SCALE * terms[s]).astype(bf16)
        total = total + dot(rows[...], rows_grad[piece, :], (0, 0))
    step = total.shape[0] // (z_size * x_size)
    starts = [(z * x_size + x) * step for x in range(x_size) for z in range(z_size)]
    grad_w[...] = jnp.concatenate([total[r : r + step] for r in starts], 0).astype(bf16)


def shards(student, proj_weight, teacher, anchors, pairs, *, sizes):
    z_size, x_size, yh_size = sizes
    n_dp = z_size * x_size * yh_size
    n_feat = lax.axis_size("feat")
    texts, features = student.shape
    width = teacher.shape[1]
    band = STEPS * texts
    rows = texts // n_feat
    share = features // n_dp
    feat = lax.axis_index("feat")

    near_student = passed_along(student, -1)
    near_teacher = passed_along(teacher, -1)
    far_student = passed_along(student, -2)
    far_teacher = passed_along(teacher, -2)

    def cost(flops):
        return pl.CostEstimate(flops=flops, bytes_accessed=3 * 10**6, transcendentals=0)

    params = pltpu.CompilerParams(vmem_limit_bytes=16 * 2**20)
    rows_type = jax.ShapeDtypeStruct((texts, width), bf16)

    proj_own, own_tiles, own_sums = pl.pallas_call(
        own_kernel,
        out_shape=(
            rows_type,
            jax.ShapeDtypeStruct((texts, 2 * texts), f32),
            jax.ShapeDtypeStruct((8, texts), f32),
        ),
        compiler_params=params,
        cost_estimate=cost(3 * 10**8),
        name="own",
    )(student, proj_weight, teacher)

    parts = pl.pallas_call(
        tile_kernel,
        out_shape=jax.ShapeDtypeStruct((n_feat, rows, (2 * STEPS + 1) * texts), f32),
        compiler_params=params,
        cost_estimate=cost(6 * 10**8),
        name="tile",
    )(
        proj_own, proj_weight, teacher, own_tiles, own_sums,
        near_student, far_student, near_teacher, far_teacher,
    )
    parts = lax.all_to_all(parts, "feat", 0, 0)

    ids = jnp.concatenate(
        [
            anchors[None] - feat * rows,
            pairs,
            lax.broadcasted_iota(jnp.int32, (1, band), 1) - feat * rows,
            jnp.zeros((4, band), jnp.int32),
        ],
        0,
    )
    tiles = pl.pallas_call(
        band_kernel,
        out_shape=jax.ShapeDtypeStruct((n_feat, rows, band + texts), bf16),
        cost_estimate=cost(10**8),
        name="band",
    )(parts, ids)
    gathered = lax.all_to_all(tiles, "feat", 0, 0)

    rows_grad, grad_w = pl.pallas_call(
        functools.partial(grad_kernel, sizes),
        out_shape=(
            jax.ShapeDtypeStruct((band, width), bf16),
            jax.ShapeDtypeStruct((features, width), bf16),
        ),
        compiler_params=params,
        cost_estimate=cost(10**9),
        name="grad",
    )(gathered, proj_weight, teacher, student, near_student, far_student)

    grad_w = lax.all_to_all(grad_w.reshape(x_size, features // x_size, width), "x", 0, 0)
    grad_w = jnp.sum(grad_w.astype(f32), 0).astype(bf16)
    grad_w = lax.all_to_all(grad_w.reshape(z_size, yh_size * share, width), "z", 0, 0)
    grad_w = jnp.sum(grad_w.astype(f32), 0)
    lower, upper = grad_w[:share], grad_w[share:]
    first = lax.axis_index("yh") == 0
    grad_w = jnp.where(first, lower, upper) + lax.ppermute(
        jnp.where(first, upper, lower), "yh", [(0, 1), (1, 0)]
    )

    height = features // n_feat
    halves = proj_weight.reshape(n_feat // 2, 2, height, width)

    def half(array, which, axis):
        return lax.dynamic_index_in_dim(array, which, axis, keepdims=False)

    def half_back(which):
        weight = half(halves, which, 1).reshape(features // 2, width)
        return dot(weight, rows_grad, (1, 1)).reshape(n_feat // 2, height, band)

    def swapped(array, bit):
        perm = [(i, i ^ (1 << bit)) for i in range(n_feat)]
        return lax.ppermute(array.astype(bf16), "feat", perm).astype(f32)

    mine = feat & 1
    back = swapped(half_back(1 - mine), 0)
    back = half_back(mine) + back
    for bit in range(1, n_feat.bit_length() - 1):
        back = back.reshape(-1, 2, height, band)
        mine = (feat >> bit) & 1
        back = half(back, mine, 1) + swapped(half(back, 1 - mine, 1), bit)
    back = back.reshape(height, band)
    grad_student = back[:, :texts]
    for s in range(1, STEPS):
        grad_student = grad_student + passed_along(back[:, s * texts : (s + 1) * texts], s)
    return (grad_w, grad_student.T)


def solution(mesh):
    n_dp, n_feat = mesh.devices.shape
    sizes = DP_SIZES[n_dp]
    split = Mesh(mesh.devices.reshape(*sizes, n_feat), (*DP, "feat"))
    return jax.shard_map(
        functools.partial(shards, sizes=sizes),
        mesh=split,
        in_specs=(P(DP, None), P(None, "feat"), P(DP, "feat"), P(DP), P(None, DP)),
        out_specs=(P(DP, "feat"), P(DP, "feat")),
        check_vma=False,
    )
```

```python
import functools

import jax
import jax.numpy as jnp
from jax import lax
from jax.experimental import pallas as pl
from jax.experimental.pallas import tpu as pltpu
from jax.sharding import Mesh, PartitionSpec as P

STEPS = 3
EPSILON = 1e-06
TEMPER = 50.0
MARGIN = 0.01
LOSS_SCALE = 1024.0

DP_SIZES = {64: (4, 8, 2), 8: (2, 2, 2)}
DP = ("z", "x", "yh")
LANES = 128
f32 = jnp.float32
bf16 = jnp.bfloat16


def dot(left, right, contract):
    return lax.dot_general(
        left, right, ((contract[:1], contract[1:]), ((), ())),
        preferred_element_type=f32,
    )


def passed_along(array, by):
    peers = lax.axis_size(DP)
    return lax.ppermute(array, DP, [(i, (i + by) % peers) for i in range(peers)])


def exact_parts(values):
    high = values.astype(bf16)
    rest = values - high.astype(f32)
    middle = rest.astype(bf16)
    low = (rest - middle.astype(f32)).astype(bf16)
    return jnp.concatenate([high, middle, low], 0)


def diagonal(size):
    return lax.broadcasted_iota(jnp.int32, (size, size), 0) == lax.broadcasted_iota(
        jnp.int32, (size, size), 1
    )


def row_sums(values):
    sums = jnp.sum(values, 1, keepdims=True)
    return jnp.sum(jnp.where(diagonal(values.shape[0]), sums, 0.0), 0, keepdims=True)


def upright(values):
    return jnp.sum(jnp.where(diagonal(values.shape[1]), values, 0.0), 1, keepdims=True)


def own_kernel(student, weight, teacher, proj_own, tiles, sums):
    texts = student.shape[0]
    own = dot(student[...], weight[...], (1, 0))
    proj_own[...] = own.astype(bf16)
    wide = teacher[...].astype(f32)
    tiles[:, :texts] = dot(proj_own[...], proj_own[...], (1, 1))
    tiles[:, texts:] = dot(teacher[...], teacher[...], (1, 1))
    sums[...] = jnp.concatenate(
        [row_sums(own * own), row_sums(wide * wide), row_sums(own * wide), jnp.zeros((5, texts), f32)],
        0,
    )


def tile_kernel(
    proj_own, weight, teacher, tiles, sums, near_student, far_student, near_teacher, far_teacher,
    payload,
):
    peers, rows, _ = payload.shape
    texts = proj_own.shape[0]
    tail = [sums[0:1, :], sums[1:2, :], sums[2:3, :]]

    def lay_out(t, tile):
        payload[:, :, t * texts : (t + 1) * texts] = tile.reshape(peers, rows, texts)

    lay_out(0, tiles[:, :texts])
    lay_out(STEPS, tiles[:, texts:])
    for s, rows_in, mates_in in (
        (1, near_student, near_teacher),
        (2, far_student, far_teacher),
    ):
        projected = dot(rows_in[...], weight[...], (1, 0))
        wide = mates_in[...].astype(f32)
        tail = tail + [row_sums(projected * projected), row_sums(wide * wide)]
        lay_out(s, dot(proj_own[...], projected.astype(bf16), (1, 1)))
        lay_out(STEPS + s, dot(teacher[...], mates_in[...], (1, 1)))
    tail = jnp.concatenate(tail + [jnp.zeros((rows - len(tail), texts), f32)], 0)
    for peer in range(peers):
        payload[peer, :, 2 * STEPS * texts :] = tail


def band_kernel(parts, ids, tiles):
    peers = tiles.shape[0]
    rows = parts.shape[1]
    band = ids.shape[1]
    texts = band // STEPS
    sums = jnp.sum(parts[...], 0)

    def part(array, t):
        return array[:, t * texts : (t + 1) * texts]

    tail = part(sums, 2 * STEPS)
    proj_sq = jnp.concatenate([tail[0:1], tail[3:4], tail[5:6]], 1)
    teach_sq = jnp.concatenate([tail[1:2], tail[4:5], tail[6:7]], 1)
    inv_proj = lax.rsqrt(proj_sq + EPSILON)
    inv_teach = lax.rsqrt(teach_sq + EPSILON)
    row_id = lax.broadcasted_iota(jnp.int32, (rows, band), 0)
    anchor = (ids[0:1, :] == row_id).astype(f32)
    own = (ids[3:4, :] == row_id).astype(f32)
    row_proj = jnp.sum(own * inv_proj, 1, keepdims=True)
    row_teach = jnp.sum(own * inv_teach, 1, keepdims=True)
    sim = sums[:, :band] * (row_proj * inv_proj)
    teach = sums[:, band : 2 * band] * (row_teach * inv_teach)
    col_id = lax.broadcasted_iota(jnp.int32, (band, band), 0)
    pick = (col_id == ids[1:2, :]).astype(f32) - (col_id == ids[2:3, :]).astype(f32)
    anchor_thrice = jnp.concatenate([anchor, anchor, anchor], 0).astype(bf16)
    gap_s = jnp.sum(dot(exact_parts(sim), anchor_thrice, (0, 0)) * pick, 0, keepdims=True)
    gap_t = jnp.sum(dot(exact_parts(teach), anchor_thrice, (0, 0)) * pick, 0, keepdims=True)
    weight = jnp.tanh(TEMPER * gap_t)
    slope = -weight * jax.nn.sigmoid(TEMPER * (MARGIN - weight * gap_s))
    added = dot(exact_parts(anchor * slope), pick.astype(bf16), (1, 1))
    grad = 2.0 * (sim - teach) + (
        added[:rows] + added[rows : 2 * rows] + added[2 * rows :]
    )
    product = grad * sim
    along = jnp.sum(product, 1, keepdims=True)
    inner = jnp.sum(product + along * own, 0, keepdims=True) * (inv_proj * inv_proj)
    both = inv_proj[:, :texts] * inv_teach[:, :texts]
    cosine = tail[2:3] * both * inv_proj[:, :texts] * inv_proj[:, :texts]
    rows_out = [
        part(inner, 0) - cosine * (1.0 / peers), part(inner, 1), part(inner, 2), both * (1.0 / peers)
    ]
    tail_id = lax.broadcasted_iota(jnp.int32, (rows, texts), 0)
    extra = jnp.zeros((rows, texts), f32)
    for r, row in enumerate(rows_out):
        high = row.astype(bf16).astype(f32)
        extra = jnp.where(tail_id == 2 * r, high, extra)
        extra = jnp.where(tail_id == 2 * r + 1, row - high, extra)
    tile = jnp.concatenate([grad * (row_proj * inv_proj), extra], 1).astype(bf16)
    for peer in range(peers):
        tiles[peer] = tile


def grad_kernel(
    sizes, core, gathered, weight, teacher, student, near_student, far_student,
    sent, kept, grad_w, rows_grad, share, sem,
):
    z_size, x_size, _ = sizes
    texts = student.shape[0]
    band = STEPS * texts
    rows_in = (student, near_student, far_student)
    projected = [dot(rows[...], weight[...], (1, 0)).astype(bf16) for rows in rows_in]
    tile = gathered[:, :, :band].reshape(texts, band)
    tail = jnp.sum(gathered[:, :, band:].astype(f32), 0)
    tail = [tail[2 * r : 2 * r + 1] + tail[2 * r + 1 : 2 * r + 2] for r in range(STEPS + 1)]
    terms = []
    for s in range(STEPS):
        tile_s = tile[:, s * texts : (s + 1) * texts]
        terms.append(dot(tile_s, projected[0], (0, 0)) - upright(tail[s]) * projected[s].astype(f32))
        terms[0] = terms[0] + dot(tile_s, projected[s], (1, 0))
    terms[0] = terms[0] - upright(tail[STEPS]) * teacher[...].astype(f32)
    total = 0.0
    for s, rows in enumerate(rows_in):
        piece = slice(s * texts, (s + 1) * texts)
        rows_grad[piece, :] = (LOSS_SCALE * terms[s]).astype(bf16)
        total = total + dot(rows[...], rows_grad[piece, :], (0, 0))
    step = total.shape[0] // (z_size * x_size)
    starts = [(z * x_size + x) * step for x in range(x_size) for z in range(z_size)]
    share[...] = jnp.concatenate([total[r : r + step] for r in starts], 0).astype(bf16)
    copy = pltpu.make_async_copy(share, grad_w, sem)
    copy.start()
    pairs, height, _ = kept.shape
    back = dot(weight[...], rows_grad[...], (1, 1)).reshape(pairs, 2, height, band)
    first = core[0] == 0
    sent[...] = jnp.where(first, back[:, 1], back[:, 0]).astype(bf16)
    kept[...] = jnp.where(first, back[:, 0], back[:, 1])
    copy.wait()


def shards(student, proj_weight, teacher, anchors, pairs, *, sizes):
    z_size, x_size, yh_size = sizes
    n_dp = z_size * x_size * yh_size
    n_feat = lax.axis_size("feat")
    texts, features = student.shape
    width = teacher.shape[1]
    band = STEPS * texts
    rows = texts // n_feat
    share = features // n_dp
    feat = lax.axis_index("feat")

    near_student = passed_along(student, -1)
    near_teacher = passed_along(teacher, -1)
    far_student = passed_along(student, -2)
    far_teacher = passed_along(teacher, -2)

    def cost(flops):
        return pl.CostEstimate(flops=flops, bytes_accessed=3 * 10**6, transcendentals=0)

    params = pltpu.CompilerParams(vmem_limit_bytes=16 * 2**20)
    rows_type = jax.ShapeDtypeStruct((texts, width), bf16)

    proj_own, own_tiles, own_sums = pl.pallas_call(
        own_kernel,
        out_shape=(
            rows_type,
            jax.ShapeDtypeStruct((texts, 2 * texts), f32),
            jax.ShapeDtypeStruct((8, texts), f32),
        ),
        compiler_params=params,
        cost_estimate=cost(3 * 10**8),
        name="own",
    )(student, proj_weight, teacher)

    parts = pl.pallas_call(
        tile_kernel,
        out_shape=jax.ShapeDtypeStruct((n_feat, rows, (2 * STEPS + 1) * texts), f32),
        compiler_params=params,
        cost_estimate=cost(6 * 10**8),
        name="tile",
    )(
        proj_own, proj_weight, teacher, own_tiles, own_sums,
        near_student, far_student, near_teacher, far_teacher,
    )
    parts = lax.all_to_all(parts, "feat", 0, 0)

    ids = jnp.concatenate(
        [
            anchors[None] - feat * rows,
            pairs,
            lax.broadcasted_iota(jnp.int32, (1, band), 1) - feat * rows,
            jnp.zeros((4, band), jnp.int32),
        ],
        0,
    )
    tiles = pl.pallas_call(
        band_kernel,
        out_shape=jax.ShapeDtypeStruct((n_feat, rows, band + texts), bf16),
        cost_estimate=cost(10**8),
        name="band",
    )(parts, ids)
    gathered = lax.all_to_all(tiles, "feat", 0, 0)

    height = features // n_feat
    half_shape = (n_feat // 2, height, band)
    vector = pl.BlockSpec(memory_space=pltpu.VMEM)
    sent, back, grad_w = pl.pallas_call(
        functools.partial(grad_kernel, sizes),
        in_specs=[pl.BlockSpec(memory_space=pltpu.SMEM)] + [vector] * 6,
        out_specs=(vector, vector, pl.BlockSpec(memory_space=pl.ANY)),
        out_shape=(
            jax.ShapeDtypeStruct(half_shape, bf16),
            jax.ShapeDtypeStruct(half_shape, f32),
            jax.ShapeDtypeStruct((features, width), bf16),
        ),
        scratch_shapes=[
            pltpu.VMEM((band, width), bf16),
            pltpu.VMEM((features, width), bf16),
            pltpu.SemaphoreType.DMA,
        ],
        compiler_params=params,
        cost_estimate=cost(10**9),
        name="grad",
    )(
        (feat & 1).astype(jnp.int32).reshape(1),
        gathered, proj_weight, teacher, student, near_student, far_student,
    )

    grad_w = lax.all_to_all(grad_w.reshape(x_size, features // x_size, width), "x", 0, 0)
    grad_w = jnp.sum(grad_w.astype(f32), 0).astype(bf16)
    grad_w = lax.all_to_all(grad_w.reshape(z_size, yh_size * share, width), "z", 0, 0)
    grad_w = jnp.sum(grad_w.astype(f32), 0)
    lower, upper = grad_w[:share], grad_w[share:]
    first = lax.axis_index("yh") == 0
    grad_w = jnp.where(first, lower, upper) + lax.ppermute(
        jnp.where(first, upper, lower), "yh", [(0, 1), (1, 0)]
    )

    def swapped(array, bit):
        perm = [(i, i ^ (1 << bit)) for i in range(n_feat)]
        return lax.ppermute(array, "feat", perm).astype(f32)

    back = back + swapped(sent, 0)
    for bit in range(1, n_feat.bit_length() - 1):
        back = back.reshape(-1, 2, height, band)
        mine = (feat >> bit) & 1
        sent = lax.dynamic_index_in_dim(back, 1 - mine, 1, keepdims=False).astype(bf16)
        back = lax.dynamic_index_in_dim(back, mine, 1, keepdims=False) + swapped(sent, bit)
    back = back.reshape(height, band)
    grad_student = back[:, :texts]
    for s in range(1, STEPS):
        grad_student = grad_student + passed_along(back[:, s * texts : (s + 1) * texts], s)
    return (grad_w, grad_student.T)


def solution(mesh):
    n_dp, n_feat = mesh.devices.shape
    sizes = DP_SIZES[n_dp]
    split = Mesh(mesh.devices.reshape(*sizes, n_feat), (*DP, "feat"))
    return jax.shard_map(
        functools.partial(shards, sizes=sizes),
        mesh=split,
        in_specs=(P(DP, None), P(None, "feat"), P(DP, "feat"), P(DP), P(None, DP)),
        out_specs=(P(DP, "feat"), P(DP, "feat")),
        check_vma=False,
    )
```

```python
import functools

import jax
import jax.numpy as jnp
from jax import lax
from jax.experimental import pallas as pl
from jax.experimental.pallas import tpu as pltpu
from jax.sharding import Mesh, PartitionSpec as P

STEPS = 3
EPSILON = 1e-06
TEMPER = 50.0
MARGIN = 0.01
LOSS_SCALE = 1024.0

DP_SIZES = {64: (4, 8, 2), 8: (2, 2, 2)}
DP = ("z", "x", "yh")
LANES = 128
f32 = jnp.float32
bf16 = jnp.bfloat16


def dot(left, right, contract):
    return lax.dot_general(
        left, right, ((contract[:1], contract[1:]), ((), ())),
        preferred_element_type=f32,
    )


def passed_along(array, by):
    peers = lax.axis_size(DP)
    return lax.ppermute(array, DP, [(i, (i + by) % peers) for i in range(peers)])


def exact_parts(values):
    high = values.astype(bf16)
    rest = values - high.astype(f32)
    middle = rest.astype(bf16)
    low = (rest - middle.astype(f32)).astype(bf16)
    return jnp.concatenate([high, middle, low], 0)


def diagonal(size):
    return lax.broadcasted_iota(jnp.int32, (size, size), 0) == lax.broadcasted_iota(
        jnp.int32, (size, size), 1
    )


def row_sums(values):
    sums = jnp.sum(values, 1, keepdims=True)
    return jnp.sum(jnp.where(diagonal(values.shape[0]), sums, 0.0), 0, keepdims=True)


def upright(values):
    return jnp.sum(jnp.where(diagonal(values.shape[1]), values, 0.0), 1, keepdims=True)


def own_kernel(student, weight, teacher, proj_own, tiles, sums):
    texts = student.shape[0]
    own = dot(student[...], weight[...], (1, 0))
    proj_own[...] = own.astype(bf16)
    wide = teacher[...].astype(f32)
    tiles[:, :texts] = dot(proj_own[...], proj_own[...], (1, 1))
    tiles[:, texts:] = dot(teacher[...], teacher[...], (1, 1))
    sums[...] = jnp.concatenate(
        [row_sums(own * own), row_sums(wide * wide), row_sums(own * wide), jnp.zeros((5, texts), f32)],
        0,
    )


def tile_kernel(
    proj_own, weight, teacher, tiles, sums, near_student, far_student, near_teacher, far_teacher,
    payload, rows_in,
):
    peers, rows, _ = payload.shape
    texts = proj_own.shape[0]
    tail = [sums[0:1, :], sums[1:2, :], sums[2:3, :]]

    def lay_out(t, tile):
        payload[:, :, t * texts : (t + 1) * texts] = tile.reshape(peers, rows, texts)

    lay_out(0, tiles[:, :texts])
    lay_out(STEPS, tiles[:, texts:])
    rows_in[:texts, :] = near_student[...]
    rows_in[texts:, :] = far_student[...]
    projected = dot(rows_in[...], weight[...], (1, 0))
    tile = dot(proj_own[...], projected.astype(bf16), (1, 1))
    squares = projected * projected
    for s, mates_in in ((1, near_teacher), (2, far_teacher)):
        piece = slice((s - 1) * texts, s * texts)
        wide = mates_in[...].astype(f32)
        tail = tail + [row_sums(squares[piece]), row_sums(wide * wide)]
        lay_out(s, tile[:, piece])
        lay_out(STEPS + s, dot(teacher[...], mates_in[...], (1, 1)))
    tail = jnp.concatenate(tail + [jnp.zeros((rows - len(tail), texts), f32)], 0)
    for peer in range(peers):
        payload[peer, :, 2 * STEPS * texts :] = tail


def band_kernel(parts, ids, tiles):
    peers = tiles.shape[0]
    rows = parts.shape[1]
    band = ids.shape[1]
    texts = band // STEPS
    sums = jnp.sum(parts[...], 0)

    def part(array, t):
        return array[:, t * texts : (t + 1) * texts]

    tail = part(sums, 2 * STEPS)
    proj_sq = jnp.concatenate([tail[0:1], tail[3:4], tail[5:6]], 1)
    teach_sq = jnp.concatenate([tail[1:2], tail[4:5], tail[6:7]], 1)
    inv_proj = lax.rsqrt(proj_sq + EPSILON)
    inv_teach = lax.rsqrt(teach_sq + EPSILON)
    row_id = lax.broadcasted_iota(jnp.int32, (rows, band), 0)
    anchor = (ids[0:1, :] == row_id).astype(f32)
    own = (ids[3:4, :] == row_id).astype(f32)
    row_proj = jnp.sum(own * inv_proj, 1, keepdims=True)
    row_teach = jnp.sum(own * inv_teach, 1, keepdims=True)
    sim = sums[:, :band] * (row_proj * inv_proj)
    teach = sums[:, band : 2 * band] * (row_teach * inv_teach)
    col_id = lax.broadcasted_iota(jnp.int32, (band, band), 0)
    pick = (col_id == ids[1:2, :]).astype(f32) - (col_id == ids[2:3, :]).astype(f32)
    anchor_thrice = jnp.concatenate([anchor, anchor, anchor], 0).astype(bf16)
    gap_s = jnp.sum(dot(exact_parts(sim), anchor_thrice, (0, 0)) * pick, 0, keepdims=True)
    gap_t = jnp.sum(dot(exact_parts(teach), anchor_thrice, (0, 0)) * pick, 0, keepdims=True)
    weight = jnp.tanh(TEMPER * gap_t)
    slope = -weight * jax.nn.sigmoid(TEMPER * (MARGIN - weight * gap_s))
    added = dot(exact_parts(anchor * slope), pick.astype(bf16), (1, 1))
    grad = 2.0 * (sim - teach) + (
        added[:rows] + added[rows : 2 * rows] + added[2 * rows :]
    )
    product = grad * sim
    along = jnp.sum(product, 1, keepdims=True)
    inner = jnp.sum(product + along * own, 0, keepdims=True) * (inv_proj * inv_proj)
    both = inv_proj[:, :texts] * inv_teach[:, :texts]
    cosine = tail[2:3] * both * inv_proj[:, :texts] * inv_proj[:, :texts]
    rows_out = [
        part(inner, 0) - cosine * (1.0 / peers), part(inner, 1), part(inner, 2), both * (1.0 / peers)
    ]
    tail_id = lax.broadcasted_iota(jnp.int32, (rows, texts), 0)
    extra = jnp.zeros((rows, texts), f32)
    for r, row in enumerate(rows_out):
        high = row.astype(bf16).astype(f32)
        extra = jnp.where(tail_id == 2 * r, high, extra)
        extra = jnp.where(tail_id == 2 * r + 1, row - high, extra)
    tile = jnp.concatenate([grad * (row_proj * inv_proj), extra], 1).astype(bf16)
    for peer in range(peers):
        tiles[peer] = tile


def grad_kernel(
    sizes, core, gathered, weight, teacher, student, near_student, far_student,
    sent, kept, grad_w, rows_in, rows_grad, share, sems,
):
    z_size, x_size, _ = sizes
    texts = student.shape[0]
    band = STEPS * texts
    for s, rows in enumerate((student, near_student, far_student)):
        rows_in[s * texts : (s + 1) * texts, :] = rows[...]
    projected = dot(rows_in[...], weight[...], (1, 0)).astype(bf16)
    tile = gathered[:, :, :band].reshape(texts, band)
    tail = jnp.sum(gathered[:, :, band:].astype(f32), 0)
    tail = [tail[2 * r : 2 * r + 1] + tail[2 * r + 1 : 2 * r + 2] for r in range(STEPS + 1)]
    scale = jnp.concatenate([upright(tail[s]) for s in range(STEPS)], 0)
    terms = dot(tile, projected[:texts], (0, 0)) - scale * projected.astype(f32)
    own = dot(tile, projected, (1, 0)) - upright(tail[STEPS]) * teacher[...].astype(f32)
    rows_grad[:texts, :] = (LOSS_SCALE * (terms[:texts] + own)).astype(bf16)
    rows_grad[texts:, :] = (LOSS_SCALE * terms[texts:]).astype(bf16)
    features, width = share.shape
    step = features // (z_size * x_size)
    starts = [(z * x_size + x) * step for x in range(x_size) for z in range(z_size)]
    copies = []
    for h in range(2):
        columns = slice(h * (width // 2), (h + 1) * (width // 2))
        total = dot(rows_in[...], rows_grad[:, columns], (0, 0))
        share[:, columns] = jnp.concatenate([total[r : r + step] for r in starts], 0).astype(bf16)
        copies.append(
            pltpu.make_async_copy(share.at[:, columns], grad_w.at[:, columns], sems.at[h])
        )
        copies[h].start()
    pairs, height, _ = kept.shape
    back = dot(weight[...], rows_grad[...], (1, 1)).reshape(pairs, 2, height, band)
    first = core[0] == 0
    sent[...] = jnp.where(first, back[:, 1], back[:, 0]).astype(bf16)
    kept[...] = jnp.where(first, back[:, 0], back[:, 1])
    for copy in copies:
        copy.wait()


def shards(student, proj_weight, teacher, anchors, pairs, *, sizes):
    z_size, x_size, yh_size = sizes
    n_dp = z_size * x_size * yh_size
    n_feat = lax.axis_size("feat")
    texts, features = student.shape
    width = teacher.shape[1]
    band = STEPS * texts
    rows = texts // n_feat
    share = features // n_dp
    feat = lax.axis_index("feat")

    near_student = passed_along(student, -1)
    near_teacher = passed_along(teacher, -1)
    far_student = passed_along(student, -2)
    far_teacher = passed_along(teacher, -2)

    def cost(flops):
        return pl.CostEstimate(flops=flops, bytes_accessed=3 * 10**6, transcendentals=0)

    params = pltpu.CompilerParams(vmem_limit_bytes=16 * 2**20)
    rows_type = jax.ShapeDtypeStruct((texts, width), bf16)

    proj_own, own_tiles, own_sums = pl.pallas_call(
        own_kernel,
        out_shape=(
            rows_type,
            jax.ShapeDtypeStruct((texts, 2 * texts), f32),
            jax.ShapeDtypeStruct((8, texts), f32),
        ),
        compiler_params=params,
        cost_estimate=cost(3 * 10**8),
        name="own",
    )(student, proj_weight, teacher)

    parts = pl.pallas_call(
        tile_kernel,
        scratch_shapes=[pltpu.VMEM(((STEPS - 1) * texts, features), bf16)],
        out_shape=jax.ShapeDtypeStruct((n_feat, rows, (2 * STEPS + 1) * texts), f32),
        compiler_params=params,
        cost_estimate=cost(6 * 10**8),
        name="tile",
    )(
        proj_own, proj_weight, teacher, own_tiles, own_sums,
        near_student, far_student, near_teacher, far_teacher,
    )
    parts = lax.all_to_all(parts, "feat", 0, 0)

    ids = jnp.concatenate(
        [
            anchors[None] - feat * rows,
            pairs,
            lax.broadcasted_iota(jnp.int32, (1, band), 1) - feat * rows,
            jnp.zeros((4, band), jnp.int32),
        ],
        0,
    )
    tiles = pl.pallas_call(
        band_kernel,
        out_shape=jax.ShapeDtypeStruct((n_feat, rows, band + texts), bf16),
        cost_estimate=cost(10**8),
        name="band",
    )(parts, ids)
    gathered = lax.all_to_all(tiles, "feat", 0, 0)

    height = features // n_feat
    half_shape = (n_feat // 2, height, band)
    vector = pl.BlockSpec(memory_space=pltpu.VMEM)
    sent, back, grad_w = pl.pallas_call(
        functools.partial(grad_kernel, sizes),
        in_specs=[pl.BlockSpec(memory_space=pltpu.SMEM)] + [vector] * 6,
        out_specs=(vector, vector, pl.BlockSpec(memory_space=pl.ANY)),
        out_shape=(
            jax.ShapeDtypeStruct(half_shape, bf16),
            jax.ShapeDtypeStruct(half_shape, f32),
            jax.ShapeDtypeStruct((features, width), bf16),
        ),
        scratch_shapes=[
            pltpu.VMEM((band, features), bf16),
            pltpu.VMEM((band, width), bf16),
            pltpu.VMEM((features, width), bf16),
            pltpu.SemaphoreType.DMA((2,)),
        ],
        compiler_params=params,
        cost_estimate=cost(10**9),
        name="grad",
    )(
        (feat & 1).astype(jnp.int32).reshape(1),
        gathered, proj_weight, teacher, student, near_student, far_student,
    )

    grad_w = lax.all_to_all(grad_w.reshape(x_size, features // x_size, width), "x", 0, 0)
    grad_w = jnp.sum(grad_w.astype(f32), 0).astype(bf16)
    grad_w = lax.all_to_all(grad_w.reshape(z_size, yh_size * share, width), "z", 0, 0)
    grad_w = jnp.sum(grad_w.astype(f32), 0)
    lower, upper = grad_w[:share], grad_w[share:]
    first = lax.axis_index("yh") == 0
    grad_w = jnp.where(first, lower, upper) + lax.ppermute(
        jnp.where(first, upper, lower), "yh", [(0, 1), (1, 0)]
    )

    def swapped(array, bit):
        perm = [(i, i ^ (1 << bit)) for i in range(n_feat)]
        return lax.ppermute(array, "feat", perm).astype(f32)

    back = back + swapped(sent, 0)
    for bit in range(1, n_feat.bit_length() - 1):
        back = back.reshape(-1, 2, height, band)
        mine = (feat >> bit) & 1
        sent = lax.dynamic_index_in_dim(back, 1 - mine, 1, keepdims=False).astype(bf16)
        back = lax.dynamic_index_in_dim(back, mine, 1, keepdims=False) + swapped(sent, bit)
    back = back.reshape(height, band)
    grad_student = back[:, :texts]
    for s in range(1, STEPS):
        grad_student = grad_student + passed_along(back[:, s * texts : (s + 1) * texts], s)
    return (grad_w, grad_student.T)


def solution(mesh):
    n_dp, n_feat = mesh.devices.shape
    sizes = DP_SIZES[n_dp]
    split = Mesh(mesh.devices.reshape(*sizes, n_feat), (*DP, "feat"))
    return jax.shard_map(
        functools.partial(shards, sizes=sizes),
        mesh=split,
        in_specs=(P(DP, None), P(None, "feat"), P(DP, "feat"), P(DP), P(None, DP)),
        out_specs=(P(DP, "feat"), P(DP, "feat")),
        check_vma=False,
    )
```

```python
import functools

import jax
import jax.numpy as jnp
from jax import lax
from jax.experimental import pallas as pl
from jax.experimental.pallas import tpu as pltpu
from jax.sharding import Mesh, PartitionSpec as P

STEPS = 3
EPSILON = 1e-06
TEMPER = 50.0
MARGIN = 0.01
LOSS_SCALE = 1024.0

DP_SIZES = {64: (4, 8, 2), 8: (2, 2, 2)}
DP = ("z", "x", "yh")
LANES = 128
f32 = jnp.float32
bf16 = jnp.bfloat16


def dot(left, right, contract):
    return lax.dot_general(
        left, right, ((contract[:1], contract[1:]), ((), ())),
        preferred_element_type=f32,
    )


def passed_along(array, by):
    peers = lax.axis_size(DP)
    return lax.ppermute(array, DP, [(i, (i + by) % peers) for i in range(peers)])


def exact_parts(values):
    high = values.astype(bf16)
    rest = values - high.astype(f32)
    middle = rest.astype(bf16)
    low = (rest - middle.astype(f32)).astype(bf16)
    return jnp.concatenate([high, middle, low], 0)


def diagonal(size):
    return lax.broadcasted_iota(jnp.int32, (size, size), 0) == lax.broadcasted_iota(
        jnp.int32, (size, size), 1
    )


def row_sums(values):
    sums = jnp.sum(values, 1, keepdims=True)
    return jnp.sum(jnp.where(diagonal(values.shape[0]), sums, 0.0), 0, keepdims=True)


def upright(values):
    return jnp.sum(jnp.where(diagonal(values.shape[1]), values, 0.0), 1, keepdims=True)


def own_kernel(student, weight, teacher, proj_own, tiles, sums):
    texts = student.shape[0]
    own = dot(student[...], weight[...], (1, 0))
    proj_own[...] = own.astype(bf16)
    wide = teacher[...].astype(f32)
    tiles[:, :texts] = dot(proj_own[...], proj_own[...], (1, 1))
    tiles[:, texts:] = dot(teacher[...], teacher[...], (1, 1))
    sums[...] = jnp.concatenate(
        [row_sums(own * own), row_sums(wide * wide), row_sums(own * wide), jnp.zeros((5, texts), f32)],
        0,
    )


def tile_kernel(
    proj_own, weight, teacher, tiles, sums, near_student, far_student, near_teacher, far_teacher,
    payload, rows_in,
):
    peers, _, texts = payload.shape
    rows = texts // peers
    tail = [sums[0:1, :], sums[1:2, :], sums[2:3, :]]

    def lay_out(t, tile):
        payload[:, t * rows : (t + 1) * rows, :] = tile.reshape(peers, rows, texts)

    lay_out(0, tiles[:, :texts])
    lay_out(STEPS, tiles[:, texts:])
    rows_in[:texts, :] = near_student[...]
    rows_in[texts:, :] = far_student[...]
    projected = dot(rows_in[...], weight[...], (1, 0))
    tile = dot(proj_own[...], projected.astype(bf16), (1, 1))
    squares = projected * projected
    for s, mates_in in ((1, near_teacher), (2, far_teacher)):
        piece = slice((s - 1) * texts, s * texts)
        wide = mates_in[...].astype(f32)
        tail = tail + [row_sums(squares[piece]), row_sums(wide * wide)]
        lay_out(s, tile[:, piece])
        lay_out(STEPS + s, dot(teacher[...], mates_in[...], (1, 1)))
    tail = jnp.concatenate(tail + [jnp.zeros((8 - len(tail), texts), f32)], 0)
    for peer in range(peers):
        payload[peer, 2 * STEPS * rows :, :] = tail


def band_kernel(parts, ids, tiles):
    peers = tiles.shape[0]
    rows = tiles.shape[1]
    band = ids.shape[1]
    texts = band // STEPS
    sums = jnp.sum(parts[...], 0)

    def part(array, t):
        return array[:, t * texts : (t + 1) * texts]

    def beside(t):
        return jnp.concatenate([sums[(t + s) * rows : (t + s + 1) * rows] for s in range(STEPS)], 1)

    tail = sums[2 * STEPS * rows :]
    proj_sq = jnp.concatenate([tail[0:1], tail[3:4], tail[5:6]], 1)
    teach_sq = jnp.concatenate([tail[1:2], tail[4:5], tail[6:7]], 1)
    inv_proj = lax.rsqrt(proj_sq + EPSILON)
    inv_teach = lax.rsqrt(teach_sq + EPSILON)
    row_id = lax.broadcasted_iota(jnp.int32, (rows, band), 0)
    anchor = (ids[0:1, :] == row_id).astype(f32)
    own = (ids[3:4, :] == row_id).astype(f32)
    row_proj = jnp.sum(own * inv_proj, 1, keepdims=True)
    row_teach = jnp.sum(own * inv_teach, 1, keepdims=True)
    sim = beside(0) * (row_proj * inv_proj)
    teach = beside(STEPS) * (row_teach * inv_teach)
    col_id = lax.broadcasted_iota(jnp.int32, (band, band), 0)
    pick = (col_id == ids[1:2, :]).astype(f32) - (col_id == ids[2:3, :]).astype(f32)
    anchor_thrice = jnp.concatenate([anchor, anchor, anchor], 0).astype(bf16)
    gap_s = jnp.sum(dot(exact_parts(sim), anchor_thrice, (0, 0)) * pick, 0, keepdims=True)
    gap_t = jnp.sum(dot(exact_parts(teach), anchor_thrice, (0, 0)) * pick, 0, keepdims=True)
    weight = jnp.tanh(TEMPER * gap_t)
    slope = -weight * jax.nn.sigmoid(TEMPER * (MARGIN - weight * gap_s))
    added = dot(exact_parts(anchor * slope), pick.astype(bf16), (1, 1))
    grad = 2.0 * (sim - teach) + (
        added[:rows] + added[rows : 2 * rows] + added[2 * rows :]
    )
    product = grad * sim
    along = jnp.sum(product, 1, keepdims=True)
    inner = jnp.sum(product + along * own, 0, keepdims=True) * (inv_proj * inv_proj)
    both = inv_proj[:, :texts] * inv_teach[:, :texts]
    cosine = tail[2:3] * both * inv_proj[:, :texts] * inv_proj[:, :texts]
    rows_out = [
        part(inner, 0) - cosine * (1.0 / peers), part(inner, 1), part(inner, 2), both * (1.0 / peers)
    ]
    tail_id = lax.broadcasted_iota(jnp.int32, (rows, texts), 0)
    extra = jnp.zeros((rows, texts), f32)
    for r, row in enumerate(rows_out):
        high = row.astype(bf16).astype(f32)
        extra = jnp.where(tail_id == 2 * r, high, extra)
        extra = jnp.where(tail_id == 2 * r + 1, row - high, extra)
    tile = jnp.concatenate([grad * (row_proj * inv_proj), extra], 1).astype(bf16)
    for peer in range(peers):
        tiles[peer] = tile


def grad_kernel(
    sizes, core, gathered, weight, teacher, student, near_student, far_student,
    sent, kept, grad_w, rows_in, rows_grad, share, sems,
):
    z_size, x_size, _ = sizes
    texts = student.shape[0]
    band = STEPS * texts
    for s, rows in enumerate((student, near_student, far_student)):
        rows_in[s * texts : (s + 1) * texts, :] = rows[...]
    projected = dot(rows_in[...], weight[...], (1, 0)).astype(bf16)
    tile = gathered[:, :, :band].reshape(texts, band)
    tail = jnp.sum(gathered[:, :, band:].astype(f32), 0)
    tail = [tail[2 * r : 2 * r + 1] + tail[2 * r + 1 : 2 * r + 2] for r in range(STEPS + 1)]
    scale = jnp.concatenate([upright(tail[s]) for s in range(STEPS)], 0)
    terms = dot(tile, projected[:texts], (0, 0)) - scale * projected.astype(f32)
    own = dot(tile, projected, (1, 0)) - upright(tail[STEPS]) * teacher[...].astype(f32)
    rows_grad[:texts, :] = (LOSS_SCALE * (terms[:texts] + own)).astype(bf16)
    rows_grad[texts:, :] = (LOSS_SCALE * terms[texts:]).astype(bf16)
    features, width = share.shape
    step = features // (z_size * x_size)
    starts = [(z * x_size + x) * step for x in range(x_size) for z in range(z_size)]
    copies = []
    for h in range(2):
        columns = slice(h * (width // 2), (h + 1) * (width // 2))
        total = dot(rows_in[...], rows_grad[:, columns], (0, 0))
        share[:, columns] = jnp.concatenate([total[r : r + step] for r in starts], 0).astype(bf16)
        copies.append(
            pltpu.make_async_copy(share.at[:, columns], grad_w.at[:, columns], sems.at[h])
        )
        copies[h].start()
    pairs, height, _ = kept.shape
    back = dot(weight[...], rows_grad[...], (1, 1)).reshape(pairs, 2, height, band)
    first = core[0] == 0
    sent[...] = jnp.where(first, back[:, 1], back[:, 0]).astype(bf16)
    kept[...] = jnp.where(first, back[:, 0], back[:, 1])
    for copy in copies:
        copy.wait()


def shards(student, proj_weight, teacher, anchors, pairs, *, sizes):
    z_size, x_size, yh_size = sizes
    n_dp = z_size * x_size * yh_size
    n_feat = lax.axis_size("feat")
    texts, features = student.shape
    width = teacher.shape[1]
    band = STEPS * texts
    rows = texts // n_feat
    share = features // n_dp
    feat = lax.axis_index("feat")

    near_student = passed_along(student, -1)
    near_teacher = passed_along(teacher, -1)
    far_student = passed_along(student, -2)
    far_teacher = passed_along(teacher, -2)

    def cost(flops):
        return pl.CostEstimate(flops=flops, bytes_accessed=3 * 10**6, transcendentals=0)

    params = pltpu.CompilerParams(vmem_limit_bytes=16 * 2**20)
    rows_type = jax.ShapeDtypeStruct((texts, width), bf16)

    proj_own, own_tiles, own_sums = pl.pallas_call(
        own_kernel,
        out_shape=(
            rows_type,
            jax.ShapeDtypeStruct((texts, 2 * texts), f32),
            jax.ShapeDtypeStruct((8, texts), f32),
        ),
        compiler_params=params,
        cost_estimate=cost(3 * 10**8),
        name="own",
    )(student, proj_weight, teacher)

    parts = pl.pallas_call(
        tile_kernel,
        scratch_shapes=[pltpu.VMEM(((STEPS - 1) * texts, features), bf16)],
        out_shape=jax.ShapeDtypeStruct((n_feat, 2 * STEPS * rows + 8, texts), f32),
        compiler_params=params,
        cost_estimate=cost(6 * 10**8),
        name="tile",
    )(
        proj_own, proj_weight, teacher, own_tiles, own_sums,
        near_student, far_student, near_teacher, far_teacher,
    )
    parts = lax.all_to_all(parts, "feat", 0, 0)

    ids = jnp.concatenate(
        [
            anchors[None] - feat * rows,
            pairs,
            lax.broadcasted_iota(jnp.int32, (1, band), 1) - feat * rows,
            jnp.zeros((4, band), jnp.int32),
        ],
        0,
    )
    tiles = pl.pallas_call(
        band_kernel,
        out_shape=jax.ShapeDtypeStruct((n_feat, rows, band + texts), bf16),
        cost_estimate=cost(10**8),
        name="band",
    )(parts, ids)
    gathered = lax.all_to_all(tiles, "feat", 0, 0)

    height = features // n_feat
    half_shape = (n_feat // 2, height, band)
    vector = pl.BlockSpec(memory_space=pltpu.VMEM)
    sent, back, grad_w = pl.pallas_call(
        functools.partial(grad_kernel, sizes),
        in_specs=[pl.BlockSpec(memory_space=pltpu.SMEM)] + [vector] * 6,
        out_specs=(vector, vector, pl.BlockSpec(memory_space=pl.ANY)),
        out_shape=(
            jax.ShapeDtypeStruct(half_shape, bf16),
            jax.ShapeDtypeStruct(half_shape, f32),
            jax.ShapeDtypeStruct((features, width), bf16),
        ),
        scratch_shapes=[
            pltpu.VMEM((band, features), bf16),
            pltpu.VMEM((band, width), bf16),
            pltpu.VMEM((features, width), bf16),
            pltpu.SemaphoreType.DMA((2,)),
        ],
        compiler_params=params,
        cost_estimate=cost(10**9),
        name="grad",
    )(
        (feat & 1).astype(jnp.int32).reshape(1),
        gathered, proj_weight, teacher, student, near_student, far_student,
    )

    grad_w = lax.all_to_all(grad_w.reshape(x_size, features // x_size, width), "x", 0, 0)
    grad_w = jnp.sum(grad_w.astype(f32), 0).astype(bf16)
    grad_w = lax.all_to_all(grad_w.reshape(z_size, yh_size * share, width), "z", 0, 0)
    grad_w = jnp.sum(grad_w.astype(f32), 0)
    lower, upper = grad_w[:share], grad_w[share:]
    first = lax.axis_index("yh") == 0
    grad_w = jnp.where(first, lower, upper) + lax.ppermute(
        jnp.where(first, upper, lower), "yh", [(0, 1), (1, 0)]
    )

    def swapped(array, bit):
        perm = [(i, i ^ (1 << bit)) for i in range(n_feat)]
        return lax.ppermute(array, "feat", perm).astype(f32)

    back = back + swapped(sent, 0)
    for bit in range(1, n_feat.bit_length() - 1):
        back = back.reshape(-1, 2, height, band)
        mine = (feat >> bit) & 1
        sent = lax.dynamic_index_in_dim(back, 1 - mine, 1, keepdims=False).astype(bf16)
        back = lax.dynamic_index_in_dim(back, mine, 1, keepdims=False) + swapped(sent, bit)
    back = back.reshape(height, band)
    grad_student = back[:, :texts]
    for s in range(1, STEPS):
        grad_student = grad_student + passed_along(back[:, s * texts : (s + 1) * texts], s)
    return (grad_w, grad_student.T)


def solution(mesh):
    n_dp, n_feat = mesh.devices.shape
    sizes = DP_SIZES[n_dp]
    split = Mesh(mesh.devices.reshape(*sizes, n_feat), (*DP, "feat"))
    return jax.shard_map(
        functools.partial(shards, sizes=sizes),
        mesh=split,
        in_specs=(P(DP, None), P(None, "feat"), P(DP, "feat"), P(DP), P(None, DP)),
        out_specs=(P(DP, "feat"), P(DP, "feat")),
        check_vma=False,
    )
```

```python
import functools

import jax
import jax.numpy as jnp
from jax import lax
from jax.experimental import pallas as pl
from jax.experimental.pallas import tpu as pltpu
from jax.sharding import Mesh, PartitionSpec as P

STEPS = 3
EPSILON = 1e-06
TEMPER = 50.0
MARGIN = 0.01
LOSS_SCALE = 1024.0

DP_SIZES = {64: (4, 8, 2), 8: (2, 2, 2)}
DP = ("z", "x", "yh")
LANES = 128
f32 = jnp.float32
bf16 = jnp.bfloat16


def dot(left, right, contract):
    return lax.dot_general(
        left, right, ((contract[:1], contract[1:]), ((), ())),
        preferred_element_type=f32,
    )


def passed_along(array, by):
    peers = lax.axis_size(DP)
    return lax.ppermute(array, DP, [(i, (i + by) % peers) for i in range(peers)])


def exact_parts(values):
    high = values.astype(bf16)
    rest = values - high.astype(f32)
    middle = rest.astype(bf16)
    low = (rest - middle.astype(f32)).astype(bf16)
    return jnp.concatenate([high, middle, low], 0)


def diagonal(size):
    return lax.broadcasted_iota(jnp.int32, (size, size), 0) == lax.broadcasted_iota(
        jnp.int32, (size, size), 1
    )


def row_sums(values):
    sums = jnp.sum(values, 1, keepdims=True)
    return jnp.sum(jnp.where(diagonal(values.shape[0]), sums, 0.0), 0, keepdims=True)


def upright(values):
    return jnp.sum(jnp.where(diagonal(values.shape[1]), values, 0.0), 1, keepdims=True)


def own_kernel(student, weight, teacher, proj_own, tiles, sums):
    texts = student.shape[0]
    own = dot(student[...], weight[...], (1, 0))
    proj_own[...] = own.astype(bf16)
    wide = teacher[...].astype(f32)
    tiles[:, :texts] = dot(proj_own[...], proj_own[...], (1, 1))
    tiles[:, texts:] = dot(teacher[...], teacher[...], (1, 1))
    sums[...] = jnp.concatenate(
        [row_sums(own * own), row_sums(wide * wide), row_sums(own * wide), jnp.zeros((5, texts), f32)],
        0,
    )


def tile_kernel(
    proj_own, weight, teacher, tiles, sums, near_student, far_student, near_teacher, far_teacher,
    payload, rows_in,
):
    peers, _, texts = payload.shape
    rows = texts // peers
    tail = [sums[0:1, :], sums[1:2, :], sums[2:3, :]]

    def lay_out(t, tile):
        payload[:, t * rows : (t + 1) * rows, :] = tile.reshape(peers, rows, texts)

    lay_out(0, tiles[:, :texts])
    lay_out(STEPS, tiles[:, texts:])
    rows_in[:texts, :] = near_student[...]
    rows_in[texts:, :] = far_student[...]
    projected = dot(rows_in[...], weight[...], (1, 0))
    tile = dot(proj_own[...], projected.astype(bf16), (1, 1))
    squares = projected * projected
    for s, mates_in in ((1, near_teacher), (2, far_teacher)):
        piece = slice((s - 1) * texts, s * texts)
        wide = mates_in[...].astype(f32)
        tail = tail + [row_sums(squares[piece]), row_sums(wide * wide)]
        lay_out(s, tile[:, piece])
        lay_out(STEPS + s, dot(teacher[...], mates_in[...], (1, 1)))
    tail = jnp.concatenate(tail + [jnp.zeros((8 - len(tail), texts), f32)], 0)
    for peer in range(peers):
        payload[peer, 2 * STEPS * rows :, :] = tail


def band_kernel(parts, ids, tiles):
    peers = tiles.shape[0]
    rows = tiles.shape[1]
    band = ids.shape[1]
    texts = band // STEPS
    sums = jnp.sum(parts[...], 0)

    def part(array, t):
        return array[:, t * texts : (t + 1) * texts]

    def beside(t):
        return jnp.concatenate([sums[(t + s) * rows : (t + s + 1) * rows] for s in range(STEPS)], 1)

    tail = sums[2 * STEPS * rows :]
    proj_sq = jnp.concatenate([tail[0:1], tail[3:4], tail[5:6]], 1)
    teach_sq = jnp.concatenate([tail[1:2], tail[4:5], tail[6:7]], 1)
    inv_proj = lax.rsqrt(proj_sq + EPSILON)
    inv_teach = lax.rsqrt(teach_sq + EPSILON)
    row_id = lax.broadcasted_iota(jnp.int32, (rows, band), 0)
    anchor = (ids[0:1, :] == row_id).astype(f32)
    own = (ids[3:4, :] == row_id).astype(f32)
    row_proj = jnp.sum(own * inv_proj, 1, keepdims=True)
    row_teach = jnp.sum(own * inv_teach, 1, keepdims=True)
    sim = beside(0) * (row_proj * inv_proj)
    teach = beside(STEPS) * (row_teach * inv_teach)
    col_id = lax.broadcasted_iota(jnp.int32, (band, band), 0)
    pick = (col_id == ids[1:2, :]).astype(f32) - (col_id == ids[2:3, :]).astype(f32)
    anchor_thrice = jnp.concatenate([anchor, anchor, anchor], 0).astype(bf16)
    gap_s = jnp.sum(dot(exact_parts(sim), anchor_thrice, (0, 0)) * pick, 0, keepdims=True)
    gap_t = jnp.sum(dot(exact_parts(teach), anchor_thrice, (0, 0)) * pick, 0, keepdims=True)
    weight = jnp.tanh(TEMPER * gap_t)
    slope = -weight * jax.nn.sigmoid(TEMPER * (MARGIN - weight * gap_s))
    added = dot(exact_parts(anchor * slope), pick.astype(bf16), (1, 1))
    grad = 2.0 * (sim - teach) + (
        added[:rows] + added[rows : 2 * rows] + added[2 * rows :]
    )
    product = grad * sim
    along = jnp.sum(product, 1, keepdims=True)
    inner = jnp.sum(product + along * own, 0, keepdims=True) * (inv_proj * inv_proj)
    both = inv_proj[:, :texts] * inv_teach[:, :texts]
    cosine = tail[2:3] * both * inv_proj[:, :texts] * inv_proj[:, :texts]
    rows_out = [
        part(inner, 0) - cosine * (1.0 / peers), part(inner, 1), part(inner, 2), both * (1.0 / peers)
    ]
    tail_id = lax.broadcasted_iota(jnp.int32, (rows, texts), 0)
    extra = jnp.zeros((rows, texts), f32)
    for r, row in enumerate(rows_out):
        high = row.astype(bf16).astype(f32)
        extra = jnp.where(tail_id == 2 * r, high, extra)
        extra = jnp.where(tail_id == 2 * r + 1, row - high, extra)
    tile = jnp.concatenate([grad * (row_proj * inv_proj), extra], 1).astype(bf16)
    for peer in range(peers):
        tiles[peer] = tile


def grad_kernel(
    sizes, core, gathered, weight, teacher, student, near_student, far_student,
    sent, kept, grad_w, rows_in, rows_grad, share, sems,
):
    z_size, x_size, _ = sizes
    texts = student.shape[0]
    band = STEPS * texts
    for s, rows in enumerate((student, near_student, far_student)):
        rows_in[s * texts : (s + 1) * texts, :] = rows[...]
    projected = dot(rows_in[...], weight[...], (1, 0)).astype(bf16)
    tile = gathered[:, :, :band].reshape(texts, band)
    tail = jnp.sum(gathered[:, :, band:].astype(f32), 0)
    tail = [tail[2 * r : 2 * r + 1] + tail[2 * r + 1 : 2 * r + 2] for r in range(STEPS + 1)]
    scale = jnp.concatenate([upright(tail[s]) for s in range(STEPS)], 0)
    terms = dot(tile, projected[:texts], (0, 0)) - scale * projected.astype(f32)
    own = dot(tile, projected, (1, 0)) - upright(tail[STEPS]) * teacher[...].astype(f32)
    rows_grad[:texts, :] = (LOSS_SCALE * (terms[:texts] + own)).astype(bf16)
    rows_grad[texts:, :] = (LOSS_SCALE * terms[texts:]).astype(bf16)
    features, width = share.shape
    step = features // (z_size * x_size)
    starts = [(z * x_size + x) * step for x in range(x_size) for z in range(z_size)]
    copies = []
    for h in range(2):
        columns = slice(h * (width // 2), (h + 1) * (width // 2))
        total = dot(rows_in[...], rows_grad[:, columns], (0, 0))
        share[:, columns] = jnp.concatenate([total[r : r + step] for r in starts], 0).astype(bf16)
        copies.append(
            pltpu.make_async_copy(share.at[:, columns], grad_w.at[:, columns], sems.at[h])
        )
        copies[h].start()
    pairs, height, _ = kept.shape
    back = dot(weight[...], rows_grad[...], (1, 1)).reshape(pairs, 2, height, band)
    first = core[0] == 0
    sent[...] = jnp.where(first, back[:, 1], back[:, 0]).astype(bf16)
    kept[...] = jnp.where(first, back[:, 0], back[:, 1])
    for copy in copies:
        copy.wait()


def shards(student, proj_weight, teacher, anchors, pairs, *, sizes):
    z_size, x_size, yh_size = sizes
    n_dp = z_size * x_size * yh_size
    n_feat = lax.axis_size("feat")
    texts, features = student.shape
    width = teacher.shape[1]
    band = STEPS * texts
    rows = texts // n_feat
    share = features // n_dp
    feat = lax.axis_index("feat")

    near_student = passed_along(student, -1)
    near_teacher = passed_along(teacher, -1)
    far_student = passed_along(student, -2)
    far_teacher = passed_along(teacher, -2)

    def cost(flops):
        return pl.CostEstimate(flops=flops, bytes_accessed=3 * 10**6, transcendentals=0)

    params = pltpu.CompilerParams(vmem_limit_bytes=16 * 2**20)
    rows_type = jax.ShapeDtypeStruct((texts, width), bf16)

    proj_own, own_tiles, own_sums = pl.pallas_call(
        own_kernel,
        out_shape=(
            rows_type,
            jax.ShapeDtypeStruct((texts, 2 * texts), f32),
            jax.ShapeDtypeStruct((8, texts), f32),
        ),
        compiler_params=params,
        cost_estimate=cost(3 * 10**8),
        name="own",
    )(student, proj_weight, teacher)

    parts = pl.pallas_call(
        tile_kernel,
        scratch_shapes=[pltpu.VMEM(((STEPS - 1) * texts, features), bf16)],
        out_shape=jax.ShapeDtypeStruct((n_feat, 2 * STEPS * rows + 8, texts), f32),
        compiler_params=params,
        cost_estimate=cost(6 * 10**8),
        name="tile",
    )(
        proj_own, proj_weight, teacher, own_tiles, own_sums,
        near_student, far_student, near_teacher, far_teacher,
    )
    parts = lax.all_to_all(parts, "feat", 0, 0)

    ids = jnp.concatenate(
        [
            anchors[None] - feat * rows,
            pairs,
            lax.broadcasted_iota(jnp.int32, (1, band), 1) - feat * rows,
            jnp.zeros((4, band), jnp.int32),
        ],
        0,
    )
    tiles = pl.pallas_call(
        band_kernel,
        out_shape=jax.ShapeDtypeStruct((n_feat, rows, band + texts), bf16),
        cost_estimate=cost(10**8),
        name="band",
    )(parts, ids)
    gathered = lax.all_to_all(tiles, "feat", 0, 0)

    height = features // n_feat
    half_shape = (n_feat // 2, height, band)
    vector = pl.BlockSpec(memory_space=pltpu.VMEM)
    sent, back, grad_w = pl.pallas_call(
        functools.partial(grad_kernel, sizes),
        in_specs=[pl.BlockSpec(memory_space=pltpu.SMEM)] + [vector] * 6,
        out_specs=(vector, vector, pl.BlockSpec(memory_space=pl.ANY)),
        out_shape=(
            jax.ShapeDtypeStruct(half_shape, bf16),
            jax.ShapeDtypeStruct(half_shape, f32),
            jax.ShapeDtypeStruct((features, width), bf16),
        ),
        scratch_shapes=[
            pltpu.VMEM((band, features), bf16),
            pltpu.VMEM((band, width), bf16),
            pltpu.VMEM((features, width), bf16),
            pltpu.SemaphoreType.DMA((2,)),
        ],
        compiler_params=params,
        cost_estimate=cost(10**9),
        name="grad",
    )(
        (feat & 1).astype(jnp.int32).reshape(1),
        gathered, proj_weight, teacher, student, near_student, far_student,
    )

    grad_w = lax.all_to_all(grad_w.reshape(x_size, features // x_size, width), "x", 0, 0)
    grad_w = jnp.sum(grad_w.astype(f32), 0).astype(bf16)
    grad_w = lax.all_to_all(grad_w.reshape(z_size, yh_size * share, width), "z", 0, 0)
    grad_w = jnp.sum(grad_w.astype(f32), 0)
    lower, upper = grad_w[:share], grad_w[share:]
    first = lax.axis_index("yh") == 0
    grad_w = jnp.where(first, lower, upper) + lax.ppermute(
        jnp.where(first, upper, lower).astype(bf16), "yh", [(0, 1), (1, 0)]
    ).astype(f32)

    def swapped(array, bit):
        perm = [(i, i ^ (1 << bit)) for i in range(n_feat)]
        return lax.ppermute(array, "feat", perm).astype(f32)

    back = back + swapped(sent, 0)
    for bit in range(1, n_feat.bit_length() - 1):
        back = back.reshape(-1, 2, height, band)
        mine = (feat >> bit) & 1
        sent = lax.dynamic_index_in_dim(back, 1 - mine, 1, keepdims=False).astype(bf16)
        back = lax.dynamic_index_in_dim(back, mine, 1, keepdims=False) + swapped(sent, bit)
    back = back.reshape(height, band)
    grad_student = back[:, :texts]
    for s in range(1, STEPS):
        terms = back[:, s * texts : (s + 1) * texts].astype(bf16)
        grad_student = grad_student + passed_along(terms, s).astype(f32)
    return (grad_w, grad_student.T)


def solution(mesh):
    n_dp, n_feat = mesh.devices.shape
    sizes = DP_SIZES[n_dp]
    split = Mesh(mesh.devices.reshape(*sizes, n_feat), (*DP, "feat"))
    return jax.shard_map(
        functools.partial(shards, sizes=sizes),
        mesh=split,
        in_specs=(P(DP, None), P(None, "feat"), P(DP, "feat"), P(DP), P(None, DP)),
        out_specs=(P(DP, "feat"), P(DP, "feat")),
        check_vma=False,
    )
```

```python
import functools

import jax
import jax.numpy as jnp
from jax import lax
from jax.experimental import pallas as pl
from jax.experimental.pallas import tpu as pltpu
from jax.sharding import Mesh, PartitionSpec as P

STEPS = 3
EPSILON = 1e-06
TEMPER = 50.0
MARGIN = 0.01
LOSS_SCALE = 1024.0

DP_SIZES = {64: (4, 8, 2), 8: (2, 2, 2)}
DP = ("z", "x", "yh")
LANES = 128
f32 = jnp.float32
bf16 = jnp.bfloat16


def dot(left, right, contract):
    return lax.dot_general(
        left, right, ((contract[:1], contract[1:]), ((), ())),
        preferred_element_type=f32,
    )


def passed_along(array, by):
    peers = lax.axis_size(DP)
    return lax.ppermute(array, DP, [(i, (i + by) % peers) for i in range(peers)])


def exact_parts(values):
    high = values.astype(bf16)
    rest = values - high.astype(f32)
    middle = rest.astype(bf16)
    low = (rest - middle.astype(f32)).astype(bf16)
    return jnp.concatenate([high, middle, low], 0)


def diagonal(size):
    return lax.broadcasted_iota(jnp.int32, (size, size), 0) == lax.broadcasted_iota(
        jnp.int32, (size, size), 1
    )


def row_sums(values):
    sums = jnp.sum(values, 1, keepdims=True)
    return jnp.sum(jnp.where(diagonal(values.shape[0]), sums, 0.0), 0, keepdims=True)


def upright(values):
    return jnp.sum(jnp.where(diagonal(values.shape[1]), values, 0.0), 1, keepdims=True)


def own_kernel(student, weight, teacher, proj_own, tiles, sums):
    texts = student.shape[0]
    own = dot(student[...], weight[...], (1, 0))
    proj_own[...] = own.astype(bf16)
    wide = teacher[...].astype(f32)
    tiles[:, :texts] = dot(proj_own[...], proj_own[...], (1, 1))
    tiles[:, texts:] = dot(teacher[...], teacher[...], (1, 1))
    sums[...] = jnp.concatenate(
        [row_sums(own * own), row_sums(wide * wide), row_sums(own * wide), jnp.zeros((5, texts), f32)],
        0,
    )


def tile_kernel(
    proj_own, weight, teacher, tiles, sums, near_student, far_student, near_teacher, far_teacher,
    payload, rows_in,
):
    peers, _, texts = payload.shape
    rows = texts // peers
    tail = [sums[0:1, :], sums[1:2, :], sums[2:3, :]]

    def lay_out(t, tile):
        payload[:, t * rows : (t + 1) * rows, :] = tile.reshape(peers, rows, texts)

    lay_out(0, tiles[:, :texts])
    lay_out(STEPS, tiles[:, texts:])
    rows_in[:texts, :] = near_student[...]
    rows_in[texts:, :] = far_student[...]
    projected = dot(rows_in[...], weight[...], (1, 0))
    tile = dot(proj_own[...], projected.astype(bf16), (1, 1))
    squares = projected * projected
    for s, mates_in in ((1, near_teacher), (2, far_teacher)):
        piece = slice((s - 1) * texts, s * texts)
        wide = mates_in[...].astype(f32)
        tail = tail + [row_sums(squares[piece]), row_sums(wide * wide)]
        lay_out(s, tile[:, piece])
        lay_out(STEPS + s, dot(teacher[...], mates_in[...], (1, 1)))
    tail = jnp.concatenate(tail + [jnp.zeros((8 - len(tail), texts), f32)], 0)
    for peer in range(peers):
        payload[peer, 2 * STEPS * rows :, :] = tail


def band_kernel(parts, ids, tiles):
    peers = tiles.shape[0]
    rows = tiles.shape[1]
    band = ids.shape[1]
    texts = band // STEPS
    sums = jnp.sum(parts[...], 0)

    def part(array, t):
        return array[:, t * texts : (t + 1) * texts]

    def beside(t):
        return jnp.concatenate([sums[(t + s) * rows : (t + s + 1) * rows] for s in range(STEPS)], 1)

    tail = sums[2 * STEPS * rows :]
    proj_sq = jnp.concatenate([tail[0:1], tail[3:4], tail[5:6]], 1)
    teach_sq = jnp.concatenate([tail[1:2], tail[4:5], tail[6:7]], 1)
    inv_proj = lax.rsqrt(proj_sq + EPSILON)
    inv_teach = lax.rsqrt(teach_sq + EPSILON)
    row_id = lax.broadcasted_iota(jnp.int32, (rows, band), 0)
    anchor = (ids[0:1, :] == row_id).astype(f32)
    own = (ids[3:4, :] == row_id).astype(f32)
    row_proj = jnp.sum(own * inv_proj, 1, keepdims=True)
    row_teach = jnp.sum(own * inv_teach, 1, keepdims=True)
    sim = beside(0) * (row_proj * inv_proj)
    teach = beside(STEPS) * (row_teach * inv_teach)
    col_id = lax.broadcasted_iota(jnp.int32, (band, band), 0)
    pick = (col_id == ids[1:2, :]).astype(f32) - (col_id == ids[2:3, :]).astype(f32)
    anchor_thrice = jnp.concatenate([anchor, anchor, anchor], 0).astype(bf16)
    gap_s = jnp.sum(dot(exact_parts(sim), anchor_thrice, (0, 0)) * pick, 0, keepdims=True)
    gap_t = jnp.sum(dot(exact_parts(teach), anchor_thrice, (0, 0)) * pick, 0, keepdims=True)
    weight = jnp.tanh(TEMPER * gap_t)
    slope = -weight * jax.nn.sigmoid(TEMPER * (MARGIN - weight * gap_s))
    added = dot(exact_parts(anchor * slope), pick.astype(bf16), (1, 1))
    grad = 2.0 * (sim - teach) + (
        added[:rows] + added[rows : 2 * rows] + added[2 * rows :]
    )
    product = grad * sim
    along = jnp.sum(product, 1, keepdims=True)
    inner = jnp.sum(product + along * own, 0, keepdims=True) * (inv_proj * inv_proj)
    both = inv_proj[:, :texts] * inv_teach[:, :texts]
    cosine = tail[2:3] * both * inv_proj[:, :texts] * inv_proj[:, :texts]
    rows_out = [
        part(inner, 0) - cosine * (1.0 / peers), part(inner, 1), part(inner, 2), both * (1.0 / peers)
    ]
    tail_id = lax.broadcasted_iota(jnp.int32, (rows, texts), 0)
    extra = jnp.zeros((rows, texts), f32)
    for r, row in enumerate(rows_out):
        high = row.astype(bf16).astype(f32)
        extra = jnp.where(tail_id == 2 * r, high, extra)
        extra = jnp.where(tail_id == 2 * r + 1, row - high, extra)
    tile = jnp.concatenate([grad * (row_proj * inv_proj), extra], 1).astype(bf16)
    for peer in range(peers):
        tiles[peer] = tile


def grad_kernel(
    sizes, core, gathered, weight, teacher, student, near_student, far_student,
    sent, kept, grad_w, rows_in, rows_grad, share, sems,
):
    z_size, x_size, _ = sizes
    texts = student.shape[0]
    band = STEPS * texts
    for s, rows in enumerate((student, near_student, far_student)):
        rows_in[s * texts : (s + 1) * texts, :] = rows[...]
    projected = dot(rows_in[...], weight[...], (1, 0)).astype(bf16)
    tile = gathered[:, :, :band].reshape(texts, band)
    tail = jnp.sum(gathered[:, :, band:].astype(f32), 0)
    tail = [tail[2 * r : 2 * r + 1] + tail[2 * r + 1 : 2 * r + 2] for r in range(STEPS + 1)]
    scale = jnp.concatenate([upright(tail[s]) for s in range(STEPS)], 0)
    terms = dot(tile, projected[:texts], (0, 0)) - scale * projected.astype(f32)
    own = dot(tile, projected, (1, 0)) - upright(tail[STEPS]) * teacher[...].astype(f32)
    rows_grad[:texts, :] = (LOSS_SCALE * (terms[:texts] + own)).astype(bf16)
    rows_grad[texts:, :] = (LOSS_SCALE * terms[texts:]).astype(bf16)
    features, width = share.shape
    step = features // (z_size * x_size)
    starts = [(z * x_size + x) * step for x in range(x_size) for z in range(z_size)]
    copies = []
    for h in range(2):
        columns = slice(h * (width // 2), (h + 1) * (width // 2))
        total = dot(rows_in[...], rows_grad[:, columns], (0, 0))
        share[:, columns] = jnp.concatenate([total[r : r + step] for r in starts], 0).astype(bf16)
        copies.append(
            pltpu.make_async_copy(share.at[:, columns], grad_w.at[:, columns], sems.at[h])
        )
        copies[h].start()
    pairs, height, _ = kept.shape
    back = dot(weight[...], rows_grad[...], (1, 1)).reshape(pairs, 2, height, band)
    first = core[0] == 0
    sent[...] = jnp.where(first, back[:, 1], back[:, 0]).astype(bf16)
    kept[...] = jnp.where(first, back[:, 0], back[:, 1])
    for copy in copies:
        copy.wait()


def shards(student, proj_weight, teacher, anchors, pairs, *, sizes):
    z_size, x_size, yh_size = sizes
    n_dp = z_size * x_size * yh_size
    n_feat = lax.axis_size("feat")
    texts, features = student.shape
    width = teacher.shape[1]
    band = STEPS * texts
    rows = texts // n_feat
    share = features // n_dp
    feat = lax.axis_index("feat")

    near_student = passed_along(student, -1)
    near_teacher = passed_along(teacher, -1)
    far_student = passed_along(student, -2)
    far_teacher = passed_along(teacher, -2)

    def cost(flops):
        return pl.CostEstimate(flops=flops, bytes_accessed=3 * 10**6, transcendentals=0)

    params = pltpu.CompilerParams(vmem_limit_bytes=16 * 2**20)
    rows_type = jax.ShapeDtypeStruct((texts, width), bf16)

    proj_own, own_tiles, own_sums = pl.pallas_call(
        own_kernel,
        out_shape=(
            rows_type,
            jax.ShapeDtypeStruct((texts, 2 * texts), f32),
            jax.ShapeDtypeStruct((8, texts), f32),
        ),
        compiler_params=params,
        cost_estimate=cost(3 * 10**8),
        name="own",
    )(student, proj_weight, teacher)

    parts = pl.pallas_call(
        tile_kernel,
        scratch_shapes=[pltpu.VMEM(((STEPS - 1) * texts, features), bf16)],
        out_shape=jax.ShapeDtypeStruct((n_feat, 2 * STEPS * rows + 8, texts), f32),
        compiler_params=params,
        cost_estimate=cost(6 * 10**8),
        name="tile",
    )(
        proj_own, proj_weight, teacher, own_tiles, own_sums,
        near_student, far_student, near_teacher, far_teacher,
    )
    parts = lax.all_to_all(parts, "feat", 0, 0)

    ids = jnp.concatenate(
        [
            anchors[None] - feat * rows,
            pairs,
            lax.broadcasted_iota(jnp.int32, (1, band), 1) - feat * rows,
            jnp.zeros((4, band), jnp.int32),
        ],
        0,
    )
    tiles = pl.pallas_call(
        band_kernel,
        out_shape=jax.ShapeDtypeStruct((n_feat, rows, band + texts), bf16),
        cost_estimate=cost(10**8),
        name="band",
    )(parts, ids)
    gathered = lax.all_to_all(tiles, "feat", 0, 0)

    height = features // n_feat
    half_shape = (n_feat // 2, height, band)
    vector = pl.BlockSpec(memory_space=pltpu.VMEM)
    sent, back, grad_w = pl.pallas_call(
        functools.partial(grad_kernel, sizes),
        in_specs=[pl.BlockSpec(memory_space=pltpu.SMEM)] + [vector] * 6,
        out_specs=(vector, vector, pl.BlockSpec(memory_space=pl.ANY)),
        out_shape=(
            jax.ShapeDtypeStruct(half_shape, bf16),
            jax.ShapeDtypeStruct(half_shape, f32),
            jax.ShapeDtypeStruct((features, width), bf16),
        ),
        scratch_shapes=[
            pltpu.VMEM((band, features), bf16),
            pltpu.VMEM((band, width), bf16),
            pltpu.VMEM((features, width), bf16),
            pltpu.SemaphoreType.DMA((2,)),
        ],
        compiler_params=params,
        cost_estimate=cost(10**9),
        name="grad",
    )(
        (feat & 1).astype(jnp.int32).reshape(1),
        gathered, proj_weight, teacher, student, near_student, far_student,
    )

    grad_w = lax.all_to_all(grad_w.reshape(x_size, features // x_size, width), "x", 0, 0)
    grad_w = jnp.sum(grad_w.astype(f32), 0).astype(bf16)
    grad_w = lax.all_to_all(grad_w.reshape(z_size, yh_size * share, width), "z", 0, 0)
    grad_w = jnp.sum(grad_w.astype(f32), 0)

    def swapped(array, bit):
        perm = [(i, i ^ (1 << bit)) for i in range(n_feat)]
        return lax.ppermute(array, "feat", perm).astype(f32)

    back = back + swapped(sent, 0)
    for bit in range(1, n_feat.bit_length() - 1):
        back = back.reshape(-1, 2, height, band)
        mine = (feat >> bit) & 1
        sent = lax.dynamic_index_in_dim(back, 1 - mine, 1, keepdims=False).astype(bf16)
        back = lax.dynamic_index_in_dim(back, mine, 1, keepdims=False) + swapped(sent, bit)
    back = back.reshape(height, band)
    moved = passed_along(back[:, texts:].astype(bf16), 2).astype(f32)
    first = lax.axis_index("yh") == 0
    to_mate = jnp.where(first, back[:, texts : 2 * texts], moved[:, :texts])
    lower, upper = grad_w[:share], grad_w[share:]
    to_mate = jnp.concatenate([jnp.where(first, upper, lower), to_mate.reshape(-1, width)], 0)
    from_mate = lax.ppermute(to_mate, "yh", [(0, 1), (1, 0)])
    grad_w = jnp.where(first, lower, upper) + from_mate[:share]
    grad_student = back[:, :texts] + moved[:, texts:] + from_mate[share:].reshape(height, texts)
    return (grad_w, grad_student.T)


def solution(mesh):
    n_dp, n_feat = mesh.devices.shape
    sizes = DP_SIZES[n_dp]
    split = Mesh(mesh.devices.reshape(*sizes, n_feat), (*DP, "feat"))
    return jax.shard_map(
        functools.partial(shards, sizes=sizes),
        mesh=split,
        in_specs=(P(DP, None), P(None, "feat"), P(DP, "feat"), P(DP), P(None, DP)),
        out_specs=(P(DP, "feat"), P(DP, "feat")),
        check_vma=False,
    )
```
